128 devices in a mesh: dp: 4 (over x), fsdp: 32 (over z, y, core).
Axes of the slice: x: 4, y: 4, z: 4, core: 2. Of those that a mesh axis runs over, the one named last changes fastest.
Arguments:
- hidden: bfloat16 [16384, 8192], P(('dp', 'fsdp')), may hold values from -6 to 6
- queries: bfloat16 [16384, 4096], P(('dp', 'fsdp')), may hold values from -170 to 170
- norm_gain: float32 [8192], replicated, may hold values from 0.1 to 1.9
- key_value_weight: bfloat16 [8192, 1024], P('fsdp'), may hold values from -0.0625 to 0.0625
- head_weight: bfloat16 [8192], replicated, may hold values from -0.0625 to 0.0625
- head_fold: bfloat16 [4096], replicated, may hold values from -0.09375 to 0.09375
- route: int32 [2, 16384], P(None, ('dp', 'fsdp')), may hold values from 0 to 127, as said below
- segments: int32 [4, 4096], P('dp'), may hold values from 0 to 7, never falling along the last dimension, each value on 1 to 2048 neighbouring positions
Outputs:
- scores: float32 [16384], P(('dp', 'fsdp'))
The draws below stay inside these ranges and needn't reach their ends.
Inputs may be any that keep to these rules, and one draw needn't show every extreme that they name: `route`: each device sends exactly 32 tokens to each of the 4 bins, all in the block of its own fsdp index, and each bin device receives exactly 32 tokens from each of 4 devices; the bin rows of all tokens are all different and fill every bin. `segments`: documents are runs of equal numbers that never fall along a bin.
All inputs are finite; a program needn't handle non-finite values.
Results may differ from the reference program's by a relative error of at most 0.0042.
Values may be sent and summed in bfloat16 or wider, within the bound.
A program may use at most 128 MiB of HBM per device.

```python
import math
import jax
import jax.numpy as jnp
import numpy as np
from jax import lax

MODEL_WIDTH = 8192
QUERY_HEADS = 32
KEY_VALUE_HEADS = 4
HEAD_SIZE = 128
TOK_DEV = 128
TOKENS = 16384
PACKED_BIN_ROWS = 4096
N_DP = 4
N_FSDP = 32


def draw_queries(key, part):
    key = jax.random.fold_in(key, 5)
    first = jax.random.fold_in(key, 0)
    shape = (TOKENS, QUERY_HEADS * HEAD_SIZE)
    value_rows = jnp.clip(jax.random.normal(first, shape, jnp.float32), -6.0, 6.0)
    return value_rows.astype(jnp.bfloat16)


def draw_route(key, part):
    key = jax.random.fold_in(key, 11)
    first, second, third = jax.random.split(key, 3)
    fanout = N_DP
    capacity = TOK_DEV // fanout
    shifts = jax.vmap(lambda item: jax.random.permutation(item, N_DP)[:fanout])(jax.random.split(first, N_FSDP))
    owned = jax.vmap(lambda item: jax.random.permutation(item, TOK_DEV))(jax.random.split(second, N_DP * N_FSDP)).reshape(N_DP, N_FSDP, TOK_DEV)
    placed = jax.vmap(lambda item: jax.random.permutation(item, TOK_DEV))(jax.random.split(third, N_DP * N_FSDP)).reshape(N_DP, N_FSDP, TOK_DEV)
    columns = jnp.arange(N_FSDP, dtype=jnp.int32)[None, :, None]
    owners = jnp.arange(N_DP, dtype=jnp.int32)[:, None, None]
    block = owned // capacity
    shift = shifts[columns, block]
    bins = (owners + shift) % N_DP
    offsets = placed[bins, columns, owned]
    return jnp.stack([bins.reshape(-1), offsets.reshape(-1)]).astype(jnp.int32)


def level_of(rng, extent, cuts, low, top_value):
    gain, own = 1.0, jax.random.fold_in(rng, 6)
    for axis_at, shards_of in cuts:
        heights = jnp.exp(jax.random.uniform(jax.random.fold_in(own, axis_at), (shards_of,), jnp.float32, low / len(cuts), top_value / len(cuts)))
        gain = gain * jnp.repeat(heights, extent[axis_at] // shards_of).reshape([-1 if axis == axis_at else 1 for axis in range(len(extent))])
    return gain


def profile(number_of, total, reach, skew):
    weights = [(1 << 20) // math.isqrt(grade ** skew) + 1 for grade in range(2, number_of + 1)]
    rest, given = total - reach - (number_of - 1), [1] * (number_of - 1)
    while rest > 0:
        movable = [i for i in range(number_of - 1) if given[i] < reach]
        pool, budget = sum([weights[i] for i in movable]), rest
        for i in movable:
            addition = min(reach - given[i], max(1, budget * weights[i] // pool), rest)
            given[i] = given[i] + addition
            rest = rest - addition
    return np.array([reach] + given)


def uneven(rng, number_of, total, limit, slope):
    if number_of == 2:
        one = jax.random.randint(rng, (), max(1, total - limit), min(limit, total - 1) + 1)
        return jnp.stack([one, total - one])
    tallies = jnp.asarray(profile(number_of, total, limit, slope), jnp.int32)
    pairs = (number_of - 1) // 2
    giver, sink = tallies[1:1 + 2 * pairs:2], tallies[2:2 + 2 * pairs:2]
    room = jnp.minimum(giver - 1, limit - sink)
    passed = jax.random.randint(jax.random.fold_in(rng, 1), (pairs,), 0, 1 << 20) % (room + 1)
    tallies = tallies.at[1:1 + 2 * pairs:2].set(giver - passed).at[2:2 + 2 * pairs:2].set(sink + passed)
    return tallies[jax.random.permutation(jax.random.fold_in(rng, 2), number_of)]


def normal_values(rng, shape, deviation, reach, pieces=(), held_as=jnp.bfloat16):
    gain = level_of(rng, shape, pieces, -0.22, 0.18) if pieces else 1.0
    result = jax.random.normal(rng, shape, jnp.float32) * deviation * gain
    return jnp.minimum(jnp.maximum(result, -reach), reach).astype(held_as)


def setup_inputs(seed: int = 0) -> dict:
    key_list = jax.random.split(jax.random.key(seed), 9)
    hidden = normal_values(key_list[0], (TOKENS, MODEL_WIDTH), 1.0, 6.0, ((0, 128),))
    queries = draw_queries(jax.random.fold_in(key_list[8], 71), 0)
    norm_gain = jnp.clip(1.0 + 0.18 * jax.random.normal(key_list[2], (MODEL_WIDTH,), jnp.float32), 0.1, 1.9)
    key_value_weight = normal_values(key_list[3], (MODEL_WIDTH, 2 * KEY_VALUE_HEADS * HEAD_SIZE), MODEL_WIDTH ** -0.5, 0.0625, ((0, 32),))
    head_weight = normal_values(key_list[4], (MODEL_WIDTH,), MODEL_WIDTH ** -0.5, 0.0625)
    head_fold = normal_values(key_list[5], (QUERY_HEADS * HEAD_SIZE,), (QUERY_HEADS * HEAD_SIZE) ** -0.5, 0.09375)
    route = draw_route(jax.random.fold_in(key_list[8], 71), 0)
    segments = jax.vmap(lambda own: jnp.searchsorted(jnp.cumsum(uneven(own, 8, PACKED_BIN_ROWS, PACKED_BIN_ROWS // 2, 2)), jnp.arange(PACKED_BIN_ROWS), side="right"))(jax.random.split(key_list[7], N_DP)).reshape((N_DP, PACKED_BIN_ROWS)).astype(jnp.int32)
    return dict(hidden=hidden, queries=queries, norm_gain=norm_gain, key_value_weight=key_value_weight, head_weight=head_weight, head_fold=head_fold, route=route, segments=segments)


def reference(hidden, queries, norm_gain, key_value_weight, head_weight, head_fold, route, segments):
    token_ids = jnp.arange(TOKENS, dtype=jnp.int32)
    column = token_ids // TOK_DEV % N_FSDP
    place = (route[0] * PACKED_BIN_ROWS + column * TOK_DEV + route[1]).astype(jnp.int32)
    bin_hidden = jnp.zeros((N_DP * PACKED_BIN_ROWS, MODEL_WIDTH), jnp.bfloat16).at[place].set(hidden).reshape(N_DP, PACKED_BIN_ROWS, MODEL_WIDTH)
    bin_queries = jnp.zeros((N_DP * PACKED_BIN_ROWS, QUERY_HEADS * HEAD_SIZE), jnp.bfloat16).at[place].set(queries).reshape(N_DP, PACKED_BIN_ROWS, QUERY_HEADS * HEAD_SIZE)
    query_group = QUERY_HEADS // KEY_VALUE_HEADS
    scale = HEAD_SIZE ** (-0.5)

    def one_bin(packed):
        rows, query_matrix, seg = packed
        widened = rows.astype(jnp.float32)
        normed = (widened * lax.rsqrt(lax.optimization_barrier(jnp.mean(widened * widened, axis=1, keepdims=True)) + 1e-05) * norm_gain).astype(jnp.bfloat16)
        key_value_pair = jnp.dot(normed, key_value_weight, preferred_element_type=jnp.float32).astype(jnp.bfloat16)
        key_rows = key_value_pair[:, :KEY_VALUE_HEADS * HEAD_SIZE].reshape(PACKED_BIN_ROWS, KEY_VALUE_HEADS, HEAD_SIZE).astype(jnp.float32)
        value_rows = key_value_pair[:, KEY_VALUE_HEADS * HEAD_SIZE:].reshape(PACKED_BIN_ROWS, KEY_VALUE_HEADS, HEAD_SIZE).astype(jnp.float32)
        head_count = query_matrix.reshape(PACKED_BIN_ROWS, KEY_VALUE_HEADS, query_group, HEAD_SIZE).astype(jnp.float32)
        logits = jnp.einsum('qgrd,kgd->grqk', head_count, key_rows) * scale
        position = jnp.arange(PACKED_BIN_ROWS, dtype=jnp.int32)
        visible = (seg[:, None] == seg[None, :]) & (position[None, :] <= position[:, None])
        logits = jnp.where(visible, logits, -1e+30)
        highest = lax.optimization_barrier(jnp.max(logits, axis=-1, keepdims=True))
        weights = jnp.where(visible, jnp.exp(logits - highest), 0.0)
        total = lax.optimization_barrier(jnp.sum(weights, axis=-1))
        rounded = weights.astype(jnp.bfloat16).astype(jnp.float32)
        attended = jnp.einsum('grqk,kgd->grqd', rounded, value_rows) / total[..., None]
        attended = jnp.transpose(attended, (2, 0, 1, 3)).reshape(PACKED_BIN_ROWS, QUERY_HEADS * HEAD_SIZE)
        residual_term = jnp.dot(rows, head_weight, preferred_element_type=jnp.float32)
        branch_term = jnp.dot(attended, head_fold.astype(jnp.float32), precision=lax.Precision.HIGHEST)
        return residual_term + branch_term
    bin_score = lax.map(one_bin, (bin_hidden, bin_queries, segments))
    return bin_score.reshape(-1)[place]
```

```python
import functools

import jax
import jax.numpy as jnp
from jax import lax
from jax.experimental import pallas as pl
from jax.experimental.pallas import tpu as pltpu
from jax.sharding import PartitionSpec as P

MESH = pl.DeviceIdType.MESH
BF = jnp.bfloat16
F32 = jnp.float32
LOG2E = 1.4426950408889634
NEG = -1e30
WROWS = 288
KROWS = 144


def nn(a, b):
    return lax.dot_general(a, b, (((1,), (0,)), ((), ())), preferred_element_type=F32)


def nt(a, b):
    return lax.dot_general(a, b, (((1,), (1,)), ((), ())), preferred_element_type=F32)


def iota(shape, axis):
    return lax.broadcasted_iota(jnp.int32, shape, axis)


def kernel(
    hid_hbm, q_hbm, gain_ref, w_hbm, hw_ref, fold_ref, route_ref, seg_ref, out_ref,
    hid, qv, wv, wpair, x3, wg, qout, qin, qx, kvout, kvin, win, kext, bias, onehot, onehot_t,
    kacc, vacc, high, acc, ret_out, ret_in,
    load_sem, pair_send, pair_recv, xs_sem, xr_sem, qs_sem, qr_sem, ks_sem, kr_sem,
    rs_sem, rr_sem, ws_sem, wr_sem, gs_sem, gr_sem,
):
    d = lax.axis_index("dp")
    f = lax.axis_index("fsdp")
    chip = f // 2
    core = f % 2
    y = chip % 4
    z = chip // 4

    def chip_at(par, u, v):
        return (1 - par) * (4 * v + u) + par * (4 * u + v)

    def coords(par):
        return (1 - par) * y + par * z, (1 - par) * z + par * y

    def near(par, du, dv):
        u, v = coords(par)
        return chip_at(par, (u + du + 4) % 4, (v + dv + 4) % 4)

    load_w = pltpu.make_async_copy(w_hbm, wv, load_sem.at[0])
    load_h = pltpu.make_async_copy(hid_hbm, hid, load_sem.at[1])
    load_q = pltpu.make_async_copy(q_hbm, qv, load_sem.at[2])
    load_w.start()
    load_h.start()
    load_q.start()

    barrier = pltpu.get_barrier_semaphore()
    peers = [(d, 2 * chip + (1 - core))]
    for dd in range(1, 4):
        for c in range(2):
            peers.append(((d + dd) % 4, 2 * chip + c))
    for du, dv in ((1, 0), (-1, 0), (0, 1), (0, -1)):
        peers.append((d, 2 * near(0, du, dv) + core))
    for peer in peers:
        pl.semaphore_signal(barrier, inc=1, device_id=peer, device_id_type=MESH)

    load_w.wait()
    fold = fold_ref[...].astype(F32)
    head_row = jnp.concatenate(
        [fold[:, h * 128 : (h + 1) * 128] for h in range(32)], axis=0
    )
    fold_t = jnp.concatenate([head_row] * 4, axis=1)
    fold_t = jnp.where(iota((32, 512), 0) // 8 == iota((32, 512), 1) // 128, fold_t, 0.0).astype(BF)
    wf = nt(fold_t, wv[:, 512:1024])
    wf_hi = wf.astype(BF).astype(F32)
    wf_lo = wf - wf_hi
    packs = []
    for c in range(2):
        rows = []
        for g in range(2):
            at = 16 * c + 8 * g
            rows += [wf_hi[at : at + 8], wf_lo[at : at + 8]]
        packs.append(jnp.concatenate(rows, axis=0).astype(BF))
    mine = pl.ds(pl.multiple_of(core * WROWS, 32), 256)
    mine_v = pl.ds(pl.multiple_of(core * WROWS + 256, 32), 32)
    own_is_1 = core == 1
    wg[chip, mine, :] = jnp.where(own_is_1, wv[:, 256:512], wv[:, 0:256])
    wg[chip, mine_v, :] = jnp.where(own_is_1, packs[1], packs[0])
    wpair[0:256, :] = jnp.where(own_is_1, wv[:, 0:256], wv[:, 256:512])
    wpair[256:288, :] = jnp.where(own_is_1, packs[0], packs[1])

    pl.semaphore_wait(barrier, len(peers))

    pair = pltpu.make_async_remote_copy(
        src_ref=wpair,
        dst_ref=wg.at[chip, pl.ds(pl.multiple_of(core * WROWS, 32), WROWS)],
        send_sem=pair_send, recv_sem=pair_recv,
        device_id=(d, 2 * chip + 1 - core), device_id_type=MESH,
    )
    pair_in = pltpu.make_async_remote_copy(
        src_ref=wpair,
        dst_ref=wg.at[chip, pl.ds(pl.multiple_of((1 - core) * WROWS, 32), WROWS)],
        send_sem=pair_send, recv_sem=pair_recv,
        device_id=(d, 2 * chip + 1 - core), device_id_type=MESH,
    )
    pair.start()

    class Gather:
        def __init__(self, buf, half, cut, send, recv):
            self.buf, self.half, self.cut = buf, half, cut
            self.sends, self.recvs = send, recv

        def part(self, par, kind):
            if kind < 2:
                off, n = 0, self.half
            elif kind == 2:
                off, n = 0, self.cut
            else:
                off, n = self.cut, self.half - self.cut
            return pl.ds(pl.multiple_of(par * self.half + off, 16), n)

        def copy(self, par, group, kind, incoming):
            step = 1 if kind in (0, 2) else -1
            hops = (1 if kind < 2 else 2) if incoming else (0 if kind < 2 else 1)
            back = -step * hops
            if group == 0:
                at = near(par, back, 0)
                to = near(par, step, 0)
            else:
                du = (0, -1, 1, 2)[group - 1]
                at = near(par, du, back)
                to = near(par, 0, step)
            ref = self.buf.at[at, self.part(par, kind)]
            return pltpu.make_async_remote_copy(
                src_ref=ref, dst_ref=ref,
                send_sem=self.sends.at[par, group, kind],
                recv_sem=self.recvs.at[par, group, kind],
                device_id=(d, 2 * to + core), device_id_type=MESH,
            )

        def send(self, par, group, kind):
            self.copy(par, group, kind, False).start()

        def wait(self, par, group, kind):
            self.copy(par, group, kind, True).wait_recv()

        def finish(self):
            for par in range(2):
                for group in range(5):
                    for kind in range(4):
                        self.copy(par, group, kind, False).wait_send()

        def begin(self, par):
            for group, kind in ((0, 0), (0, 1), (1, 0), (1, 1)):
                self.send(par, group, kind)

        def step1(self):
            for kind in range(2):
                for par in range(2):
                    self.wait(par, 0, kind)
                    self.send(par, 2 + kind, 0)
                    self.send(par, 2 + kind, 1)
                    self.send(par, 0, 2 + kind)

        def step2(self):
            for kind in range(2):
                for par in range(2):
                    self.wait(par, 1, kind)
                    self.send(par, 1, 2 + kind)

        def step3(self):
            for par in range(2):
                self.wait(par, 0, 2)
                self.wait(par, 0, 3)
                self.send(par, 4, 0)
                self.send(par, 4, 1)

        def step4(self):
            for group in (2, 3):
                for kind in range(2):
                    for par in range(2):
                        self.wait(par, group, kind)
                        self.send(par, group, 2 + kind)

        def step5(self):
            for kind in range(2):
                for par in range(2):
                    self.wait(par, 4, kind)
                    self.send(par, 4, 2 + kind)

        def step6(self, group):
            for par in range(2):
                self.wait(par, group, 2)
                self.wait(par, group, 3)

    weights = Gather(wg, WROWS, WROWS // 2, ws_sem, wr_sem)
    keys = Gather(win, KROWS, 80, gs_sem, gr_sem)

    weights.begin(core)
    pair_in.wait_recv()
    weights.begin(1 - core)

    route = route_ref[...]
    bins = jnp.broadcast_to(route[0:1, :], (128, 128))
    offs = jnp.broadcast_to(route[1:2, :], (128, 128))
    i0 = iota((128, 128), 0)
    i1 = iota((128, 128), 1)
    member = (bins == i0).astype(F32)
    before = (i0 < i1).astype(BF)
    count = nn(member.astype(BF), before)
    rank = jnp.sum(member * count, axis=0, keepdims=True)
    slot = route[0:1, :].astype(F32) * 32.0 + rank
    perm = (jnp.broadcast_to(slot, (128, 128)) == i0.astype(F32)).astype(BF)
    eye = i0 == i1
    off_col = jnp.sum(jnp.where(eye, offs.astype(F32), 0.0), axis=1, keepdims=True)
    bin_col = jnp.sum(jnp.where(eye, bins.astype(F32), 0.0), axis=1, keepdims=True)
    rank_col = jnp.sum(jnp.where(eye, jnp.broadcast_to(rank, (128, 128)), 0.0), axis=1, keepdims=True)

    load_q.wait()
    off_sorted = nn(perm, jnp.broadcast_to(off_col, (128, 128)).astype(BF)).astype(BF)
    for c in range(2):
        for b in range(4):
            qout[b, c, :, 2048:2176] = off_sorted[b * 32 : (b + 1) * 32]

    def sort_q(i, _):
        for c in range(2):
            src = pl.ds(pl.multiple_of(c * 2048 + i * 256, 256), 256)
            dst = pl.ds(pl.multiple_of(i * 256, 256), 256)
            block = nn(perm, qv[:, src]).astype(BF)
            for b in range(4):
                qout[b, c, :, dst] = block[b * 32 : (b + 1) * 32]
        return 0

    lax.fori_loop(0, 8, sort_q, 0)

    def q_copy(dd, c):
        b = (d + dd) % 4
        to = (core + c) % 2
        n = dd * 2 + c
        return pltpu.make_async_remote_copy(
            src_ref=qout.at[b, to], dst_ref=qin.at[d, core],
            send_sem=qs_sem.at[n], recv_sem=qr_sem.at[n],
            device_id=(b, 2 * chip + to), device_id_type=MESH,
        )

    def q_arrival(dd, c):
        n = dd * 2 + c
        return pltpu.make_async_remote_copy(
            src_ref=qout.at[d, core], dst_ref=qin.at[(d - dd + 4) % 4, (core + c) % 2],
            send_sem=qs_sem.at[n], recv_sem=qr_sem.at[n],
            device_id=(d, 2 * chip + 1 - core), device_id_type=MESH,
        )

    q_pairs = [(dd, c) for dd in range(4) for c in range(2) if dd or c]
    for dd, c in q_pairs:
        q_copy(dd, c).start()
    qin[d, core] = qout[d, core]

    load_h.wait()

    def squares(i, carry):
        total, dot = carry
        at = pl.ds(pl.multiple_of(i * 256, 256), 256)
        x = hid[:, at].astype(F32)
        return total + x * x, dot + x * hw_ref[:, at].astype(F32)

    zero = jnp.zeros((128, 256), F32)
    total, dot = lax.fori_loop(0, 32, squares, (zero, zero))
    root = lax.rsqrt(jnp.sum(total, axis=1, keepdims=True) * (1.0 / 8192.0) + 1e-05)
    residual = jnp.sum(dot, axis=1, keepdims=True)
    my_rows = pl.ds(pl.multiple_of(core * 128, 128), 128)

    def normalise(i, _):
        at = pl.ds(pl.multiple_of(i * 256, 256), 256)
        normed = (hid[:, at].astype(F32) * root * gain_ref[:, at]).astype(BF)
        x3[i, my_rows, :] = nn(perm, normed).astype(BF)
        return 0

    lax.fori_loop(0, 32, normalise, 0)
    x_rows = x3.at[:, my_rows, :]
    x_copy = pltpu.make_async_remote_copy(
        src_ref=x_rows, dst_ref=x_rows, send_sem=xs_sem, recv_sem=xr_sem,
        device_id=(d, 2 * chip + 1 - core), device_id_type=MESH,
    )
    other_rows = x3.at[:, pl.ds(pl.multiple_of((1 - core) * 128, 128), 128), :]
    x_in = pltpu.make_async_remote_copy(
        src_ref=other_rows, dst_ref=other_rows, send_sem=xs_sem, recv_sem=xr_sem,
        device_id=(d, 2 * chip + 1 - core), device_id_type=MESH,
    )
    x_copy.start()
    weights.step1()

    def segment_keys(i, _):
        at = pl.ds(pl.multiple_of(i * 256, 256), 256)
        s = jnp.broadcast_to(seg_ref[:, at], (128, 256))
        k = iota((128, 256), 0)
        part = jnp.where((k < 8) & (s != k), NEG, 0.0)
        kext[i] = part.T.astype(BF)
        return 0

    lax.fori_loop(0, 16, segment_keys, 0)

    x_in.wait_recv()
    kacc[...] = jnp.zeros_like(kacc)
    vacc[...] = jnp.zeros_like(vacc)

    def project(par, du, dv):
        c = near(par, du, dv)
        x = x3[2 * c + par]
        base = par * WROWS
        kacc[...] += nn(x, wg[c, pl.ds(pl.multiple_of(base, 32), 256), :])
        vacc[...] += nt(wg[c, pl.ds(pl.multiple_of(base + 256, 32), 32), :], x)

    def project_all(places):
        for du, dv in places:
            def body(par, _, du=du, dv=dv):
                project(par, du, dv)
                return 0

            lax.fori_loop(0, 2, body, 0)

    project_all([(0, 0), (-1, 0), (1, 0)])
    weights.step2()
    weights.step3()
    project_all([(0, -1), (0, 1), (2, 0)])
    weights.step4()
    project_all([(-1, -1), (-1, 1), (1, -1), (1, 1)])
    weights.step5()
    project_all([(2, -1), (2, 1)])

    for dd, c in q_pairs:
        q_arrival(dd, c).wait_recv()
    off = qin[:, :, :, 2048:2176].reshape(256, 128).astype(F32)
    arrival = iota((256, 128), 0)
    place = off + ((arrival // 32) % 2).astype(F32) * 128.0
    place = jnp.concatenate([place, place], axis=1)
    hot = (place == iota((256, 256), 1).astype(F32)).astype(F32)
    onehot[...] = hot.astype(BF)
    onehot_t[...] = hot.T.astype(BF)
    own_at = pl.ds(pl.multiple_of(chip * 256, 256), 256)
    seg_hot = (jnp.broadcast_to(seg_ref[:, own_at], (128, 256)) == iota((128, 256), 0)).astype(BF)
    qseg = nt(onehot[...], seg_hot).astype(BF)
    later = jnp.where(iota((256, 256), 0) > iota((256, 256), 1), NEG, 0.0).astype(BF)
    bias[...] = nt(later, onehot[...])
    for h in range(16):
        qx[h, :, 0:128] = qin[:, :, :, h * 128 : (h + 1) * 128].reshape(256, 128)
        qx[h, :, 128:256] = qseg

    for group, place_of in ((1, (0, 2)), (2, (-1, 2)), (3, (1, 2)), (4, (2, 2))):
        weights.step6(group)
        project_all([place_of])

    k_rows = kacc[...].astype(BF)
    v = vacc[...]
    v_rows = []
    for g in range(2):
        vf = v[g * 16 : g * 16 + 8] + v[g * 16 + 8 : g * 16 + 16]
        vf_hi = vf.astype(BF).astype(F32)
        v_rows += [vf_hi, vf - vf_hi]
    v_rows.append(jnp.zeros((96, 256), F32))
    v_cols = jnp.concatenate(v_rows, axis=0).T.astype(BF)
    for s in range(2):
        for b in range(4):
            at = s * 128 + b * 32
            kvout[b, s, :, 0:256] = k_rows[at : at + 32]
            kvout[b, s, :, 256:384] = v_cols[at : at + 32]

    def k_copy(dd):
        b = (d + dd) % 4
        return pltpu.make_async_remote_copy(
            src_ref=kvout.at[b], dst_ref=kvin.at[d],
            send_sem=ks_sem.at[dd], recv_sem=kr_sem.at[dd],
            device_id=(b, f), device_id_type=MESH,
        )

    def k_arrival(dd):
        return pltpu.make_async_remote_copy(
            src_ref=kvout.at[d], dst_ref=kvin.at[(d - dd + 4) % 4],
            send_sem=ks_sem.at[dd], recv_sem=kr_sem.at[dd],
            device_id=((d + dd) % 4, f), device_id_type=MESH,
        )

    for dd in range(1, 4):
        k_copy(dd).start()
    kvin[d] = kvout[d]
    for dd in range(1, 4):
        k_arrival(dd).wait_recv()

    got_k = kvin[:, :, :, 0:256].reshape(256, 256)
    got_v = kvin[:, :, :, 256:384].reshape(256, 128).astype(F32).T[0:32].astype(BF)
    win[chip, 0:256, :] = nn(onehot_t[...], got_k).astype(BF)
    win[chip, 256:288, :] = nn(got_v, onehot[...]).astype(BF)
    keys.begin(0)
    keys.begin(1)

    scale = LOG2E * 128.0 ** -0.5
    ones = jnp.ones((16, 256), BF)

    def attend(c, first):
        ext = kext[c]
        for g in range(2):
            key = jnp.concatenate([win[c, 0:256, g * 128 : (g + 1) * 128], ext], axis=1)
            val = jnp.concatenate([win[c, 256 + 16 * g : 272 + 16 * g, :], ones], axis=0)

            def heads(i, _, g=g, key=key, val=val):
                for j in range(2):
                    h = g * 8 + i * 2 + j
                    s = nt(key, qx[h])
                    if first:
                        s = s + bias[...]
                        new = jnp.max(s, axis=0, keepdims=True)
                        p = jnp.exp2((s - new) * scale).astype(BF)
                        acc[h] = nn(val, p)
                    else:
                        old = high[h]
                        new = jnp.maximum(old, jnp.max(s, axis=0, keepdims=True))
                        p = jnp.exp2((s - new) * scale).astype(BF)
                        acc[h] = acc[h] * jnp.exp2((old - new) * scale) + nn(val, p)
                    high[h] = new
                return 0

            lax.fori_loop(0, 4, heads, 0)

    def attend_near(dy, dz):
        c = near(0, dy, dz)

        @pl.when((c < chip) & (c >= chip - 8))
        def _():
            attend(c, False)

    attend(chip, True)
    keys.step1()
    keys.step2()
    keys.step3()
    keys.step4()
    keys.step5()
    for group in range(1, 5):
        keys.step6(group)
    for dy in range(4):
        for dz in range(4):
            if dy or dz:
                attend_near(dy, dz)

    branch = jnp.zeros((1, 256), F32)
    for h in range(16):
        a = acc[h]
        j = h % 8
        branch = branch + (a[j : j + 1] + a[8 + j : 9 + j]) / a[16:17]
    ret_out[...] = jnp.broadcast_to(branch, (8, 256))

    def r_copy(dd, c):
        n = dd * 2 + c
        return pltpu.make_async_remote_copy(
            src_ref=ret_out, dst_ref=ret_in.at[d, core],
            send_sem=rs_sem.at[n], recv_sem=rr_sem.at[n],
            device_id=((d + dd) % 4, 2 * chip + (core + c) % 2), device_id_type=MESH,
        )

    def r_arrival(dd, c):
        n = dd * 2 + c
        return pltpu.make_async_remote_copy(
            src_ref=ret_out, dst_ref=ret_in.at[(d - dd + 4) % 4, (core + c) % 2],
            send_sem=rs_sem.at[n], recv_sem=rr_sem.at[n],
            device_id=(d, 2 * chip + 1 - core), device_id_type=MESH,
        )

    for dd, c in q_pairs:
        r_copy(dd, c).start()
    ret_in[d, core] = ret_out[...]
    for dd, c in q_pairs:
        r_arrival(dd, c).wait_recv()

    lane = (d * 64 + core * 32).astype(F32) + rank_col
    lanes = iota((128, 256), 1).astype(F32)
    value = jnp.zeros((128, 256), F32)
    for b in range(4):
        row = ret_in[b, 0][0:1] + ret_in[b, 1][0:1]
        value = value + jnp.where((lanes == lane) & (bin_col == float(b)), row, 0.0)
    score = jnp.sum(value, axis=1, keepdims=True) + residual
    out_ref[...] = jnp.sum(jnp.where(eye, score, 0.0), axis=0, keepdims=True)

    pair.wait_send()
    x_copy.wait_send()
    weights.finish()
    keys.finish()
    for dd, c in q_pairs:
        q_copy(dd, c).wait_send()
        r_copy(dd, c).wait_send()
    for dd in range(1, 4):
        k_copy(dd).wait_send()


def on_device(
    hidden, queries, norm_gain, key_value_weight, head_weight, head_fold, route, segments
):
    vmem = pl.BlockSpec(memory_space=pltpu.VMEM)
    hbm = pl.BlockSpec(memory_space=pl.ANY)
    dma = pltpu.SemaphoreType.DMA
    out = pl.pallas_call(
        kernel,
        out_shape=jax.ShapeDtypeStruct((1, 128), F32),
        in_specs=[hbm, hbm, vmem, hbm, vmem, vmem, vmem, vmem],
        out_specs=vmem,
        scratch_shapes=[
            pltpu.VMEM((128, 8192), BF),
            pltpu.VMEM((128, 4096), BF),
            pltpu.VMEM((256, 1024), BF),
            pltpu.VMEM((WROWS, 256), BF),
            pltpu.VMEM((32, 256, 256), BF),
            pltpu.VMEM((16, 2 * WROWS, 256), BF),
            pltpu.VMEM((4, 2, 32, 2176), BF),
            pltpu.VMEM((4, 2, 32, 2176), BF),
            pltpu.VMEM((16, 256, 256), BF),
            pltpu.VMEM((4, 2, 32, 384), BF),
            pltpu.VMEM((4, 2, 32, 384), BF),
            pltpu.VMEM((16, 2 * KROWS, 256), BF),
            pltpu.VMEM((16, 256, 128), BF),
            pltpu.VMEM((256, 256), F32),
            pltpu.VMEM((256, 256), BF),
            pltpu.VMEM((256, 256), BF),
            pltpu.VMEM((256, 256), F32),
            pltpu.VMEM((32, 256), F32),
            pltpu.VMEM((16, 1, 256), F32),
            pltpu.VMEM((16, 32, 256), F32),
            pltpu.VMEM((8, 256), F32),
            pltpu.VMEM((4, 2, 8, 256), F32),
            dma((3,)),
            dma, dma, dma, dma,
            dma((8,)), dma((8,)),
            dma((4,)), dma((4,)),
            dma((8,)), dma((8,)),
            dma((2, 5, 4)), dma((2, 5, 4)),
            dma((2, 5, 4)), dma((2, 5, 4)),
        ],
        compiler_params=pltpu.CompilerParams(
            collective_id=0, has_side_effects=True, vmem_limit_bytes=48 * 1024 * 1024
        ),
        cost_estimate=pl.CostEstimate(
            flops=10_000_000_000, bytes_accessed=4_000_000, transcendentals=10_000_000
        ),
    )(
        hidden, queries, norm_gain.reshape(1, -1), key_value_weight,
        head_weight.reshape(1, -1), head_fold.reshape(1, -1), route, segments,
    )
    return out.reshape(-1)


def solution(mesh):
    in_specs = (
        P(("dp", "fsdp"), None),
        P(("dp", "fsdp"), None),
        P(),
        P("fsdp", None),
        P(),
        P(),
        P(None, ("dp", "fsdp")),
        P("dp", None),
    )
    out_specs = P(("dp", "fsdp"))
    return jax.shard_map(
        on_device, mesh=mesh, in_specs=in_specs, out_specs=out_specs, check_vma=False
    )
```

```python
import functools

import jax
import jax.numpy as jnp
from jax import lax
from jax.experimental import pallas as pl
from jax.experimental.pallas import tpu as pltpu
from jax.sharding import PartitionSpec as P

MESH = pl.DeviceIdType.MESH
BF = jnp.bfloat16
F32 = jnp.float32
LOG2E = 1.4426950408889634
NEG = -1e30
WROWS = 288
KROWS = 144


def nn(a, b):
    return lax.dot_general(a, b, (((1,), (0,)), ((), ())), preferred_element_type=F32)


def nt(a, b):
    return lax.dot_general(a, b, (((1,), (1,)), ((), ())), preferred_element_type=F32)


def iota(shape, axis):
    return lax.broadcasted_iota(jnp.int32, shape, axis)


def kernel(
    hid_hbm, q_hbm, gain_hbm, w_hbm, hw_hbm, fold_hbm, route_hbm, seg_hbm, out_ref,
    gain_ref, hw_ref, fold_ref, route_ref, seg_ref, hw_row, hid, qv, wv, wpair, x3, wg, qout, qin, qx, kvout, kvin, win, kext, bias, onehot, onehot_t,
    kacc, vacc, high, acc, sbuf, ret_out, ret_in,
    load_sem, pair_send, pair_recv, xs_sem, xr_sem, qs_sem, qr_sem, ks_sem, kr_sem,
    rs_sem, rr_sem, ws_sem, wr_sem, gs_sem, gr_sem,
):
    d = lax.axis_index("dp")
    f = lax.axis_index("fsdp")
    chip = f // 2
    core = f % 2
    y = chip % 4
    z = chip // 4

    def chip_at(par, u, v):
        return (1 - par) * (4 * v + u) + par * (4 * u + v)

    def coords(par):
        return (1 - par) * y + par * z, (1 - par) * z + par * y

    def near(par, du, dv):
        u, v = coords(par)
        return chip_at(par, (u + du + 4) % 4, (v + dv + 4) % 4)

    loads = [
        pltpu.make_async_copy(src, dst, load_sem.at[n])
        for n, (src, dst) in enumerate([
            (w_hbm, wv), (fold_hbm, fold_ref), (route_hbm, route_ref), (q_hbm, qv),
            (hid_hbm, hid), (hw_hbm, hw_ref), (gain_hbm, gain_ref), (seg_hbm, seg_ref),
        ])
    ]
    load_w, load_fold, load_route, load_q, load_h, load_hw, load_gain, load_seg = loads
    for load in loads:
        load.start()

    barrier = pltpu.get_barrier_semaphore()
    peers = [(d, 2 * chip + (1 - core))]
    for dd in range(1, 4):
        for c in range(2):
            peers.append(((d + dd) % 4, 2 * chip + c))
    for du, dv in ((1, 0), (-1, 0), (0, 1), (0, -1)):
        peers.append((d, 2 * near(0, du, dv) + core))
    for peer in peers:
        pl.semaphore_signal(barrier, inc=1, device_id=peer, device_id_type=MESH)

    load_w.wait()
    load_fold.wait()
    fold = fold_ref[...].reshape(1, 4096).astype(F32)
    head_row = jnp.concatenate(
        [fold[:, h * 128 : (h + 1) * 128] for h in range(32)], axis=0
    )
    fold_t = jnp.concatenate([head_row] * 4, axis=1)
    fold_t = jnp.where(iota((32, 512), 0) // 8 == iota((32, 512), 1) // 128, fold_t, 0.0).astype(BF)
    wf = nt(fold_t, wv[:, 512:1024])
    wf_hi = wf.astype(BF).astype(F32)
    wf_lo = wf - wf_hi
    packs = []
    for c in range(2):
        rows = []
        for g in range(2):
            at = 16 * c + 8 * g
            rows += [wf_hi[at : at + 8], wf_lo[at : at + 8]]
        packs.append(jnp.concatenate(rows, axis=0).astype(BF))
    mine = pl.ds(pl.multiple_of(core * WROWS, 32), 256)
    mine_v = pl.ds(pl.multiple_of(core * WROWS + 256, 32), 32)
    own_is_1 = core == 1
    wg[chip, mine, :] = jnp.where(own_is_1, wv[:, 256:512], wv[:, 0:256])
    wg[chip, mine_v, :] = jnp.where(own_is_1, packs[1], packs[0])
    wpair[0:256, :] = jnp.where(own_is_1, wv[:, 0:256], wv[:, 256:512])
    wpair[256:288, :] = jnp.where(own_is_1, packs[0], packs[1])

    pl.semaphore_wait(barrier, len(peers))

    pair = pltpu.make_async_remote_copy(
        src_ref=wpair,
        dst_ref=wg.at[chip, pl.ds(pl.multiple_of(core * WROWS, 32), WROWS)],
        send_sem=pair_send, recv_sem=pair_recv,
        device_id=(d, 2 * chip + 1 - core), device_id_type=MESH,
    )
    pair_in = pltpu.make_async_remote_copy(
        src_ref=wpair,
        dst_ref=wg.at[chip, pl.ds(pl.multiple_of((1 - core) * WROWS, 32), WROWS)],
        send_sem=pair_send, recv_sem=pair_recv,
        device_id=(d, 2 * chip + 1 - core), device_id_type=MESH,
    )
    pair.start()

    class Gather:
        def __init__(self, buf, half, cut, send, recv):
            self.buf, self.half, self.cut = buf, half, cut
            self.sends, self.recvs = send, recv

        def part(self, par, kind):
            if kind < 2:
                off, n = 0, self.half
            elif kind == 2:
                off, n = 0, self.cut
            else:
                off, n = self.cut, self.half - self.cut
            return pl.ds(pl.multiple_of(par * self.half + off, 16), n)

        def copy(self, par, group, kind, incoming):
            step = 1 if kind in (0, 2) else -1
            hops = (1 if kind < 2 else 2) if incoming else (0 if kind < 2 else 1)
            back = -step * hops
            if group == 0:
                at = near(par, back, 0)
                to = near(par, step, 0)
            else:
                du = (0, -1, 1, 2)[group - 1]
                at = near(par, du, back)
                to = near(par, 0, step)
            ref = self.buf.at[at, self.part(par, kind)]
            return pltpu.make_async_remote_copy(
                src_ref=ref, dst_ref=ref,
                send_sem=self.sends.at[par, group, kind],
                recv_sem=self.recvs.at[par, group, kind],
                device_id=(d, 2 * to + core), device_id_type=MESH,
            )

        def send(self, par, group, kind):
            self.copy(par, group, kind, False).start()

        def wait(self, par, group, kind):
            self.copy(par, group, kind, True).wait_recv()

        def finish(self):
            for par in range(2):
                for group in range(5):
                    for kind in range(4):
                        self.copy(par, group, kind, False).wait_send()

        def begin(self, par):
            for group, kind in ((0, 0), (0, 1), (1, 0), (1, 1)):
                self.send(par, group, kind)

        def step1(self):
            for kind in range(2):
                for par in range(2):
                    self.wait(par, 0, kind)
                    self.send(par, 2 + kind, 0)
                    self.send(par, 2 + kind, 1)
                    self.send(par, 0, 2 + kind)

        def step2(self):
            for kind in range(2):
                for par in range(2):
                    self.wait(par, 1, kind)
                    self.send(par, 1, 2 + kind)

        def step3(self):
            for par in range(2):
                self.wait(par, 0, 2)
                self.wait(par, 0, 3)
                self.send(par, 4, 0)
                self.send(par, 4, 1)

        def step4(self):
            for group in (2, 3):
                for kind in range(2):
                    for par in range(2):
                        self.wait(par, group, kind)
                        self.send(par, group, 2 + kind)

        def step5(self):
            for kind in range(2):
                for par in range(2):
                    self.wait(par, 4, kind)
                    self.send(par, 4, 2 + kind)

        def step6(self, group):
            for par in range(2):
                self.wait(par, group, 2)
                self.wait(par, group, 3)

    weights = Gather(wg, WROWS, WROWS // 2, ws_sem, wr_sem)
    keys = Gather(win, KROWS, 80, gs_sem, gr_sem)

    weights.begin(core)
    pair_in.wait_recv()
    weights.begin(1 - core)

    load_route.wait()
    route = route_ref[...]
    bins = jnp.broadcast_to(route[0:1, :], (128, 128))
    offs = jnp.broadcast_to(route[1:2, :], (128, 128))
    i0 = iota((128, 128), 0)
    i1 = iota((128, 128), 1)
    member = (bins == i0).astype(F32)
    before = (i0 < i1).astype(BF)
    count = nn(member.astype(BF), before)
    rank = jnp.sum(member * count, axis=0, keepdims=True)
    slot = route[0:1, :].astype(F32) * 32.0 + rank
    perm = (jnp.broadcast_to(slot, (128, 128)) == i0.astype(F32)).astype(BF)
    eye = i0 == i1
    off_col = jnp.sum(jnp.where(eye, offs.astype(F32), 0.0), axis=1, keepdims=True)
    bin_col = jnp.sum(jnp.where(eye, bins.astype(F32), 0.0), axis=1, keepdims=True)
    rank_col = jnp.sum(jnp.where(eye, jnp.broadcast_to(rank, (128, 128)), 0.0), axis=1, keepdims=True)

    load_q.wait()
    off_sorted = nn(perm, jnp.broadcast_to(off_col, (128, 128)).astype(BF)).astype(BF)
    for c in range(2):
        for b in range(4):
            qout[b, c, :, 2048:2176] = off_sorted[b * 32 : (b + 1) * 32]

    def sort_q(i, _):
        for c in range(2):
            src = pl.ds(pl.multiple_of(c * 2048 + i * 256, 256), 256)
            dst = pl.ds(pl.multiple_of(i * 256, 256), 256)
            block = nn(perm, qv[:, src]).astype(BF)
            for b in range(4):
                qout[b, c, :, dst] = block[b * 32 : (b + 1) * 32]
        return 0

    lax.fori_loop(0, 8, sort_q, 0)

    def q_copy(dd, c):
        b = (d + dd) % 4
        to = (core + c) % 2
        n = dd * 2 + c
        return pltpu.make_async_remote_copy(
            src_ref=qout.at[b, to], dst_ref=qin.at[d, core],
            send_sem=qs_sem.at[n], recv_sem=qr_sem.at[n],
            device_id=(b, 2 * chip + to), device_id_type=MESH,
        )

    def q_arrival(dd, c):
        n = dd * 2 + c
        return pltpu.make_async_remote_copy(
            src_ref=qout.at[d, core], dst_ref=qin.at[(d - dd + 4) % 4, (core + c) % 2],
            send_sem=qs_sem.at[n], recv_sem=qr_sem.at[n],
            device_id=(d, 2 * chip + 1 - core), device_id_type=MESH,
        )

    q_pairs = [(dd, c) for dd in range(4) for c in range(2) if dd or c]
    for dd, c in q_pairs:
        q_copy(dd, c).start()
    qin[d, core] = qout[d, core]

    load_h.wait()
    load_hw.wait()
    load_gain.wait()
    load_seg.wait()
    hw_row[...] = hw_ref[...].reshape(1, 8192).astype(F32)

    def squares(i, carry):
        total, dot = carry
        at = pl.ds(pl.multiple_of(i * 256, 256), 256)
        x = hid[:, at].astype(F32)
        return total + x * x, dot + x * hw_row[:, at]

    zero = jnp.zeros((128, 256), F32)
    total, dot = lax.fori_loop(0, 32, squares, (zero, zero))
    root = lax.rsqrt(jnp.sum(total, axis=1, keepdims=True) * (1.0 / 8192.0) + 1e-05)
    residual = jnp.sum(dot, axis=1, keepdims=True)
    my_rows = pl.ds(pl.multiple_of(core * 128, 128), 128)

    def normalise(i, _):
        at = pl.ds(pl.multiple_of(i * 256, 256), 256)
        normed = (hid[:, at].astype(F32) * root * gain_ref[:, at]).astype(BF)
        x3[i, my_rows, :] = nn(perm, normed).astype(BF)
        return 0

    lax.fori_loop(0, 32, normalise, 0)
    x_rows = x3.at[:, my_rows, :]
    x_copy = pltpu.make_async_remote_copy(
        src_ref=x_rows, dst_ref=x_rows, send_sem=xs_sem, recv_sem=xr_sem,
        device_id=(d, 2 * chip + 1 - core), device_id_type=MESH,
    )
    other_rows = x3.at[:, pl.ds(pl.multiple_of((1 - core) * 128, 128), 128), :]
    x_in = pltpu.make_async_remote_copy(
        src_ref=other_rows, dst_ref=other_rows, send_sem=xs_sem, recv_sem=xr_sem,
        device_id=(d, 2 * chip + 1 - core), device_id_type=MESH,
    )
    x_copy.start()
    weights.step1()

    def segment_keys(i, _):
        at = pl.ds(pl.multiple_of(i * 256, 256), 256)
        s = jnp.broadcast_to(seg_ref[:, at], (128, 256))
        k = iota((128, 256), 0)
        part = jnp.where((k < 8) & (s != k), NEG, 0.0)
        kext[i] = part.T.astype(BF)
        return 0

    lax.fori_loop(0, 16, segment_keys, 0)

    x_in.wait_recv()
    kacc[...] = jnp.zeros_like(kacc)
    vacc[...] = jnp.zeros_like(vacc)

    def project(par, du, dv):
        c = near(par, du, dv)
        x = x3[2 * c + par]
        base = par * WROWS
        kacc[...] += nn(x, wg[c, pl.ds(pl.multiple_of(base, 32), 256), :])
        vacc[...] += nt(wg[c, pl.ds(pl.multiple_of(base + 256, 32), 32), :], x)

    def project_all(places):
        for du, dv in places:
            def body(par, _, du=du, dv=dv):
                project(par, du, dv)
                return 0

            lax.fori_loop(0, 2, body, 0)

    project_all([(0, 0), (-1, 0), (1, 0)])
    weights.step2()
    weights.step3()
    project_all([(0, -1), (0, 1), (2, 0)])
    weights.step4()
    project_all([(-1, -1), (-1, 1), (1, -1), (1, 1)])
    weights.step5()
    project_all([(2, -1), (2, 1)])

    for dd, c in q_pairs:
        q_arrival(dd, c).wait_recv()
    off = qin[:, :, :, 2048:2176].reshape(256, 128).astype(F32)
    arrival = iota((256, 128), 0)
    place = off + ((arrival // 32) % 2).astype(F32) * 128.0
    place = jnp.concatenate([place, place], axis=1)
    hot = (place == iota((256, 256), 1).astype(F32)).astype(F32)
    onehot[...] = hot.astype(BF)
    onehot_t[...] = hot.T.astype(BF)
    own_at = pl.ds(pl.multiple_of(chip * 256, 256), 256)
    seg_hot = (jnp.broadcast_to(seg_ref[:, own_at], (128, 256)) == iota((128, 256), 0)).astype(BF)
    qseg = nt(seg_hot, onehot[...]).astype(BF)
    later = jnp.where(iota((256, 256), 0) > iota((256, 256), 1), NEG, 0.0).astype(BF)
    bias[...] = nt(later, onehot[...])
    for h in range(16):
        qh = qin[:, :, :, h * 128 : (h + 1) * 128].reshape(256, 128)
        qx[h, 0:128, :] = qh.astype(F32).T.astype(BF)
        qx[h, 128:256, :] = qseg

    for group, place_of in ((1, (0, 2)), (2, (-1, 2)), (3, (1, 2)), (4, (2, 2))):
        weights.step6(group)
        project_all([place_of])

    k_rows = kacc[...].astype(BF)
    v = vacc[...]
    v_rows = []
    for g in range(2):
        vf = v[g * 16 : g * 16 + 8] + v[g * 16 + 8 : g * 16 + 16]
        vf_hi = vf.astype(BF).astype(F32)
        v_rows += [vf_hi, vf - vf_hi]
    v_rows.append(jnp.zeros((96, 256), F32))
    v_cols = jnp.concatenate(v_rows, axis=0).T.astype(BF)
    for s in range(2):
        for b in range(4):
            at = s * 128 + b * 32
            kvout[b, s, :, 0:256] = k_rows[at : at + 32]
            kvout[b, s, :, 256:384] = v_cols[at : at + 32]

    def k_copy(dd):
        b = (d + dd) % 4
        return pltpu.make_async_remote_copy(
            src_ref=kvout.at[b], dst_ref=kvin.at[d],
            send_sem=ks_sem.at[dd], recv_sem=kr_sem.at[dd],
            device_id=(b, f), device_id_type=MESH,
        )

    def k_arrival(dd):
        return pltpu.make_async_remote_copy(
            src_ref=kvout.at[d], dst_ref=kvin.at[(d - dd + 4) % 4],
            send_sem=ks_sem.at[dd], recv_sem=kr_sem.at[dd],
            device_id=((d + dd) % 4, f), device_id_type=MESH,
        )

    for dd in range(1, 4):
        k_copy(dd).start()
    kvin[d] = kvout[d]
    for dd in range(1, 4):
        k_arrival(dd).wait_recv()

    got_k = kvin[:, :, :, 0:256].reshape(256, 256)
    got_v = kvin[:, :, :, 256:384].reshape(256, 128).astype(F32).T[0:32].astype(BF)
    win[chip, 0:256, :] = nn(onehot_t[...], got_k).astype(BF)
    win[chip, 256:288, :] = nn(got_v, onehot[...]).astype(BF)
    keys.begin(0)
    keys.begin(1)

    scale = LOG2E * 128.0 ** -0.5
    ones = jnp.ones((16, 256), BF)

    def attend(c, first):
        def scores(h):
            g = h // 8
            key = jnp.concatenate([win[c, 0:256, g * 128 : (g + 1) * 128], kext[c]], axis=1)
            s = nn(key, qx[h])
            sbuf[h % 8] = s + bias[...] if first else s

        for h in range(4):
            scores(h)
        for batch in range(0, 16, 4):
            for h in range(batch + 4, min(batch + 8, 16)):
                scores(h)
            for h in range(batch, batch + 4):
                g = h // 8
                val = jnp.concatenate([win[c, 256 + 16 * g : 272 + 16 * g, :], ones], axis=0)
                s = sbuf[h % 8]
                new = jnp.max(s, axis=0, keepdims=True)
                if not first:
                    old = high[h]
                    new = jnp.maximum(old, new)
                p = jnp.exp2((s - new) * scale).astype(BF)
                part = nn(val, p)
                acc[h] = part if first else acc[h] * jnp.exp2((old - new) * scale) + part
                high[h] = new

    def attend_list(count, place):
        def body(i, _):
            dy, dz = place(i)
            c = near(0, dy, dz)

            @pl.when((c < chip) & (c >= chip - 8))
            def _():
                attend(c, False)

            return 0

        lax.fori_loop(0, count, body, 0)

    attend(chip, True)
    keys.step1()
    keys.step2()
    keys.step3()
    attend_list(4, lambda i: ((1 - 2 * (i % 2)) * (1 - i // 2), (1 - 2 * (i % 2)) * (i // 2)))
    keys.step4()
    keys.step5()
    attend_list(4, lambda i: (1 - 2 * (i % 2), 1 - 2 * (i // 2)))
    for group in range(1, 5):
        keys.step6(group)
    attend_list(7, lambda i: (
        2 * (1 - i // 4) + (i - 5) * (i // 4), (i - 1) * (1 - i // 4) + 2 * (i // 4)
    ))

    branch = jnp.zeros((1, 256), F32)
    for h in range(16):
        a = acc[h]
        j = h % 8
        branch = branch + (a[j : j + 1] + a[8 + j : 9 + j]) / a[16:17]
    ret_out[...] = jnp.broadcast_to(branch, (8, 256))

    def r_copy(dd, c):
        n = dd * 2 + c
        return pltpu.make_async_remote_copy(
            src_ref=ret_out, dst_ref=ret_in.at[d, core],
            send_sem=rs_sem.at[n], recv_sem=rr_sem.at[n],
            device_id=((d + dd) % 4, 2 * chip + (core + c) % 2), device_id_type=MESH,
        )

    def r_arrival(dd, c):
        n = dd * 2 + c
        return pltpu.make_async_remote_copy(
            src_ref=ret_out, dst_ref=ret_in.at[(d - dd + 4) % 4, (core + c) % 2],
            send_sem=rs_sem.at[n], recv_sem=rr_sem.at[n],
            device_id=(d, 2 * chip + 1 - core), device_id_type=MESH,
        )

    for dd, c in q_pairs:
        r_copy(dd, c).start()
    ret_in[d, core] = ret_out[...]
    for dd, c in q_pairs:
        r_arrival(dd, c).wait_recv()

    lane = (d * 64 + core * 32).astype(F32) + rank_col
    lanes = iota((128, 256), 1).astype(F32)
    value = jnp.zeros((128, 256), F32)
    for b in range(4):
        row = ret_in[b, 0][0:1] + ret_in[b, 1][0:1]
        value = value + jnp.where((lanes == lane) & (bin_col == float(b)), row, 0.0)
    score = jnp.sum(value, axis=1, keepdims=True) + residual
    out_ref[...] = jnp.sum(jnp.where(eye, score, 0.0), axis=0, keepdims=True)

    pair.wait_send()
    x_copy.wait_send()
    weights.finish()
    keys.finish()
    for dd, c in q_pairs:
        q_copy(dd, c).wait_send()
        r_copy(dd, c).wait_send()
    for dd in range(1, 4):
        k_copy(dd).wait_send()


def on_device(
    hidden, queries, norm_gain, key_value_weight, head_weight, head_fold, route, segments
):
    vmem = pl.BlockSpec(memory_space=pltpu.VMEM)
    hbm = pl.BlockSpec(memory_space=pl.ANY)
    dma = pltpu.SemaphoreType.DMA
    out = pl.pallas_call(
        kernel,
        out_shape=jax.ShapeDtypeStruct((1, 128), F32),
        in_specs=[hbm] * 8,
        out_specs=vmem,
        scratch_shapes=[
            pltpu.VMEM((1, 8192), F32),
            pltpu.VMEM((8192,), BF),
            pltpu.VMEM((4096,), BF),
            pltpu.VMEM((2, 128), jnp.int32),
            pltpu.VMEM((1, 4096), jnp.int32),
            pltpu.VMEM((1, 8192), F32),
            pltpu.VMEM((128, 8192), BF),
            pltpu.VMEM((128, 4096), BF),
            pltpu.VMEM((256, 1024), BF),
            pltpu.VMEM((WROWS, 256), BF),
            pltpu.VMEM((32, 256, 256), BF),
            pltpu.VMEM((16, 2 * WROWS, 256), BF),
            pltpu.VMEM((4, 2, 32, 2176), BF),
            pltpu.VMEM((4, 2, 32, 2176), BF),
            pltpu.VMEM((16, 256, 256), BF),
            pltpu.VMEM((4, 2, 32, 384), BF),
            pltpu.VMEM((4, 2, 32, 384), BF),
            pltpu.VMEM((16, 2 * KROWS, 256), BF),
            pltpu.VMEM((16, 256, 128), BF),
            pltpu.VMEM((256, 256), F32),
            pltpu.VMEM((256, 256), BF),
            pltpu.VMEM((256, 256), BF),
            pltpu.VMEM((256, 256), F32),
            pltpu.VMEM((32, 256), F32),
            pltpu.VMEM((16, 1, 256), F32),
            pltpu.VMEM((16, 32, 256), F32),
            pltpu.VMEM((8, 256, 256), F32),
            pltpu.VMEM((8, 256), F32),
            pltpu.VMEM((4, 2, 8, 256), F32),
            dma((8,)),
            dma, dma, dma, dma,
            dma((8,)), dma((8,)),
            dma((4,)), dma((4,)),
            dma((8,)), dma((8,)),
            dma((2, 5, 4)), dma((2, 5, 4)),
            dma((2, 5, 4)), dma((2, 5, 4)),
        ],
        compiler_params=pltpu.CompilerParams(
            collective_id=0, has_side_effects=True, vmem_limit_bytes=62 * 1024 * 1024
        ),
        cost_estimate=pl.CostEstimate(
            flops=10_000_000_000, bytes_accessed=4_000_000, transcendentals=10_000_000
        ),
    )(
        hidden, queries, norm_gain.reshape(1, -1), key_value_weight,
        head_weight, head_fold, route, segments,
    )
    return out.reshape(-1)


def solution(mesh):
    in_specs = (
        P(("dp", "fsdp"), None),
        P(("dp", "fsdp"), None),
        P(),
        P("fsdp", None),
        P(),
        P(),
        P(None, ("dp", "fsdp")),
        P("dp", None),
    )
    out_specs = P(("dp", "fsdp"))
    return jax.shard_map(
        on_device, mesh=mesh, in_specs=in_specs, out_specs=out_specs, check_vma=False
    )
```

```python
import functools

import jax
import jax.numpy as jnp
from jax import lax
from jax.experimental import pallas as pl
from jax.experimental.pallas import tpu as pltpu
from jax.sharding import PartitionSpec as P

MESH = pl.DeviceIdType.MESH
BF = jnp.bfloat16
F32 = jnp.float32
LOG2E = 1.4426950408889634
NEG = -1e30
WROWS = 288
KROWS = 144


def nn(a, b):
    return lax.dot_general(a, b, (((1,), (0,)), ((), ())), preferred_element_type=F32)


def nt(a, b):
    return lax.dot_general(a, b, (((1,), (1,)), ((), ())), preferred_element_type=F32)


def iota(shape, axis):
    return lax.broadcasted_iota(jnp.int32, shape, axis)


def kernel(
    hid_hbm, q_hbm, gain_hbm, w_hbm, hw_hbm, fold_hbm, route_hbm, seg_hbm, out_ref,
    gain_ref, hw_ref, fold_ref, route_ref, seg_ref, hw_row, hid, qv, wv, wpair, x3, wg, qout, qin, qx, kvout, kvin, win, kext, bias, onehot, onehot_t,
    kacc, vacc, high, acc, sbuf, ret_out, ret_in,
    load_sem, pair_send, pair_recv, xs_sem, xr_sem, qs_sem, qr_sem, ks_sem, kr_sem,
    rs_sem, rr_sem, ws_sem, wr_sem, gs_sem, gr_sem,
):
    d = lax.axis_index("dp")
    f = lax.axis_index("fsdp")
    chip = f // 2
    core = f % 2
    y = chip % 4
    z = chip // 4

    def chip_at(par, u, v):
        return (1 - par) * (4 * v + u) + par * (4 * u + v)

    def coords(par):
        return (1 - par) * y + par * z, (1 - par) * z + par * y

    def near(par, du, dv):
        u, v = coords(par)
        return chip_at(par, (u + du + 4) % 4, (v + dv + 4) % 4)

    barrier = pltpu.get_barrier_semaphore()
    peers = [(d, 2 * chip + (1 - core))]
    for dd in range(1, 4):
        for c in range(2):
            peers.append(((d + dd) % 4, 2 * chip + c))
    for du, dv in ((1, 0), (-1, 0), (0, 1), (0, -1), (2, 0), (0, 2)):
        peers.append((d, 2 * near(0, du, dv) + core))
    for peer in peers:
        pl.semaphore_signal(barrier, inc=1, device_id=peer, device_id_type=MESH)

    loads = [
        pltpu.make_async_copy(src, dst, load_sem.at[n])
        for n, (src, dst) in enumerate([
            (w_hbm, wv), (fold_hbm, fold_ref), (route_hbm, route_ref), (q_hbm, qv),
            (hid_hbm, hid), (hw_hbm, hw_ref), (gain_hbm, gain_ref), (seg_hbm, seg_ref),
        ])
    ]
    load_w, load_fold, load_route, load_q, load_h, load_hw, load_gain, load_seg = loads
    for load in loads:
        load.start()

    load_w.wait()
    load_fold.wait()
    fold = fold_ref[...].reshape(1, 4096).astype(F32)
    head_row = jnp.concatenate(
        [fold[:, h * 128 : (h + 1) * 128] for h in range(32)], axis=0
    )
    fold_t = jnp.concatenate([head_row] * 4, axis=1)
    fold_t = jnp.where(iota((32, 512), 0) // 8 == iota((32, 512), 1) // 128, fold_t, 0.0).astype(BF)
    wf = nt(fold_t, wv[:, 512:1024])
    wf_hi = wf.astype(BF).astype(F32)
    wf_lo = wf - wf_hi
    own_is_1 = core == 1
    for g in range(2):
        packs = []
        for c in range(2):
            at = 16 * c + 8 * g
            rows = [wf_hi[at : at + 8], wf_lo[at : at + 8]]
            pack = jnp.concatenate(rows, axis=0).astype(BF)
            packs.append((wv[:, (2 * c + g) * 128 : (2 * c + g + 1) * 128], pack))
        base = pl.multiple_of(core * WROWS, 32)
        for n in range(2):
            mine = jnp.where(own_is_1, packs[1][n], packs[0][n])
            theirs = jnp.where(own_is_1, packs[0][n], packs[1][n])
            if n == 0:
                wg[g, chip, pl.ds(base, 256), :] = mine
                wpair[g, 0:256, :] = theirs
            else:
                for side in range(2):
                    lanes_of = slice(side * 128, (side + 1) * 128)
                    at = 256 + 16 * side
                    wg[g, chip, pl.ds(base + at, 16), :] = mine[:, lanes_of]
                    wpair[g, at : at + 16, :] = theirs[:, lanes_of]

    pl.semaphore_wait(barrier, len(peers))

    def pair(g, side):
        at = pl.ds(pl.multiple_of(side * WROWS, 32), WROWS)
        return pltpu.make_async_remote_copy(
            src_ref=wpair.at[g], dst_ref=wg.at[g, chip, at],
            send_sem=pair_send.at[g], recv_sem=pair_recv.at[g],
            device_id=(d, 2 * chip + 1 - core), device_id_type=MESH,
        )

    for g in range(2):
        pair(g, core).start()

    class Gather:
        def __init__(self, g):
            self.g, self.half, self.cut = g, WROWS, WROWS // 2

        def part(self, par, kind):
            if kind < 2:
                off, n = 0, self.half
            elif kind == 2:
                off, n = 0, self.cut
            else:
                off, n = self.cut, self.half - self.cut
            return pl.ds(pl.multiple_of(par * self.half + off, 16), n)

        def copy(self, par, group, kind, incoming):
            step = 1 if kind in (0, 2) else -1
            hops = (1 if kind < 2 else 2) if incoming else (0 if kind < 2 else 1)
            back = -step * hops
            if group == 0:
                at = near(par, back, 0)
                to = near(par, step, 0)
            else:
                du = (0, -1, 1, 2)[group - 1]
                at = near(par, du, back)
                to = near(par, 0, step)
            ref = wg.at[self.g, at, self.part(par, kind)]
            return pltpu.make_async_remote_copy(
                src_ref=ref, dst_ref=ref,
                send_sem=ws_sem.at[self.g, par, group, kind],
                recv_sem=wr_sem.at[self.g, par, group, kind],
                device_id=(d, 2 * to + core), device_id_type=MESH,
            )

        def send(self, par, group, kind):
            self.copy(par, group, kind, False).start()

        def wait(self, par, group, kind):
            self.copy(par, group, kind, True).wait_recv()

        def finish(self):
            for par in range(2):
                for group in range(5):
                    for kind in range(4):
                        self.copy(par, group, kind, False).wait_send()

        def begin(self, par, group):
            self.send(par, group, 0)
            self.send(par, group, 1)

        def step1(self):
            for kind in range(2):
                for par in range(2):
                    self.wait(par, 0, kind)
                    self.send(par, 2 + kind, 0)
                    self.send(par, 2 + kind, 1)
                    self.send(par, 0, 2 + kind)

        def step2(self):
            for kind in range(2):
                for par in range(2):
                    self.wait(par, 1, kind)
                    self.send(par, 1, 2 + kind)

        def step3(self):
            for par in range(2):
                self.wait(par, 0, 2)
                self.wait(par, 0, 3)
                self.send(par, 4, 0)
                self.send(par, 4, 1)

        def step4(self):
            for group in (2, 3):
                for kind in range(2):
                    for par in range(2):
                        self.wait(par, group, kind)
                        self.send(par, group, 2 + kind)

        def step5(self):
            for kind in range(2):
                for par in range(2):
                    self.wait(par, 4, kind)
                    self.send(par, 4, 2 + kind)

        def step6(self, group):
            for par in range(2):
                self.wait(par, group, 2)
                self.wait(par, group, 3)

    class Keys:
        def __init__(self, g):
            self.g = g

        def copy(self, n, at, par, to):
            ref = win.at[self.g, at, pl.ds(par * KROWS, KROWS)]
            return pltpu.make_async_remote_copy(
                src_ref=ref, dst_ref=ref,
                send_sem=gs_sem.at[self.g, n], recv_sem=gr_sem.at[self.g, n],
                device_id=(d, 2 * to + core), device_id_type=MESH,
            )

        def first_y(self, e, incoming):
            at = near(0, -e if incoming else 0, 0)
            return self.copy(e - 1, at, 0, near(0, e, 0)), True

        def first_z(self, j, incoming):
            at = near(0, 0, -j if incoming else 0)
            return self.copy(2 + j, at, 1, near(0, 0, j)), (z >= j if incoming else z < 4 - j)

        def then_z(self, k, j, incoming):
            at = near(0, k, -j if incoming else 0)
            ok = z >= j if incoming else z < 4 - j
            if j == 2:
                ok = ok & ((y + k) % 4 >= y)
            return self.copy(5 + 2 * k + j - 1, at, 0, near(0, 0, j)), ok

        def then_y(self, e, j, incoming):
            at = near(0, -e if incoming else 0, -j)
            source = (y - e + 4) % 4 if incoming else y
            target = y if incoming else (y + e) % 4
            ok = z >= j
            if j == 0:
                ok = source < target
            if j == 2:
                ok = ok & (source >= target)
            return self.copy(13 + 3 * j + e - 1, at, 1, near(0, e, 0)), ok

        def run(self, act, made):
            copy, ok = made
            if ok is True:
                act(copy)
            else:
                @pl.when(ok)
                def _():
                    act(copy)

        def send(self, kind, *which):
            self.run(lambda copy: copy.start(), kind(*which, False))

        def wait(self, kind, *which):
            self.run(lambda copy: copy.wait_recv(), kind(*which, True))

        def begin(self):
            for e in (1, 3, 2):
                self.send(self.first_y, e)
            for j in (1, 2):
                self.send(self.first_z, j)
            for j in (1, 2):
                self.send(self.then_z, 0, j)
            for e in (1, 3, 2):
                self.send(self.then_y, e, 0)

        def forward(self):
            self.wait(self.first_z, 1)
            for e in (1, 3, 2):
                self.send(self.then_y, e, 1)
            for e in (1, 3, 2):
                self.wait(self.first_y, e)
                for j in (1, 2):
                    self.send(self.then_z, (4 - e) % 4, j)
            self.wait(self.first_z, 2)
            for e in (1, 3, 2):
                self.send(self.then_y, e, 2)

        def row(self, j):
            for e in (1, 3, 2):
                self.wait(self.then_y, e, j)
            if j:
                for k in range(4):
                    self.wait(self.then_z, k, j)

        def finish(self):
            done = lambda copy: copy.wait_send()
            for e in (1, 2, 3):
                self.run(done, self.first_y(e, False))
                for j in range(3):
                    self.run(done, self.then_y(e, j, False))
            for j in (1, 2):
                self.run(done, self.first_z(j, False))
                for k in range(4):
                    self.run(done, self.then_z(k, j, False))

    weights = [Gather(0), Gather(1)]
    keys = [Keys(0), Keys(1)]

    for g in range(2):
        for group in range(2):
            if g == 0 or group == 0:
                weights[g].begin(core, group)
        pair(g, 1 - core).wait_recv()
        for group in range(2):
            if g == 0 or group == 0:
                weights[g].begin(1 - core, group)

    load_route.wait()
    route = route_ref[...]
    bins = jnp.broadcast_to(route[0:1, :], (128, 128))
    offs = jnp.broadcast_to(route[1:2, :], (128, 128))
    i0 = iota((128, 128), 0)
    i1 = iota((128, 128), 1)
    member = (bins == i0).astype(F32)
    before = (i0 < i1).astype(BF)
    count = nn(member.astype(BF), before)
    rank = jnp.sum(member * count, axis=0, keepdims=True)
    slot = route[0:1, :].astype(F32) * 32.0 + rank
    perm = (jnp.broadcast_to(slot, (128, 128)) == i0.astype(F32)).astype(BF)
    eye = i0 == i1
    off_col = jnp.sum(jnp.where(eye, offs.astype(F32), 0.0), axis=1, keepdims=True)
    bin_col = jnp.sum(jnp.where(eye, bins.astype(F32), 0.0), axis=1, keepdims=True)
    rank_col = jnp.sum(jnp.where(eye, jnp.broadcast_to(rank, (128, 128)), 0.0), axis=1, keepdims=True)

    load_q.wait()
    off_sorted = nn(perm, jnp.broadcast_to(off_col, (128, 128)).astype(BF)).astype(BF)
    for c in range(2):
        for b in range(4):
            qout[b, c, :, 2048:2176] = off_sorted[b * 32 : (b + 1) * 32]

    def sort_q(i, _):
        for c in range(2):
            src = pl.ds(pl.multiple_of(c * 2048 + i * 256, 256), 256)
            dst = pl.ds(pl.multiple_of(i * 256, 256), 256)
            block = nn(perm, qv[:, src]).astype(BF)
            for b in range(4):
                qout[b, c, :, dst] = block[b * 32 : (b + 1) * 32]
        return 0

    lax.fori_loop(0, 8, sort_q, 0)

    def q_copy(dd, c):
        b = (d + dd) % 4
        to = (core + c) % 2
        n = dd * 2 + c
        return pltpu.make_async_remote_copy(
            src_ref=qout.at[b, to], dst_ref=qin.at[d, core],
            send_sem=qs_sem.at[n], recv_sem=qr_sem.at[n],
            device_id=(b, 2 * chip + to), device_id_type=MESH,
        )

    def q_arrival(dd, c):
        n = dd * 2 + c
        return pltpu.make_async_remote_copy(
            src_ref=qout.at[d, core], dst_ref=qin.at[(d - dd + 4) % 4, (core + c) % 2],
            send_sem=qs_sem.at[n], recv_sem=qr_sem.at[n],
            device_id=(d, 2 * chip + 1 - core), device_id_type=MESH,
        )

    q_pairs = [(dd, c) for dd in range(4) for c in range(2) if dd or c]
    for dd, c in q_pairs:
        q_copy(dd, c).start()
    qin[d, core] = qout[d, core]

    weights[0].step1()
    for par in range(2):
        weights[1].begin(par, 1)

    load_h.wait()
    load_hw.wait()
    load_gain.wait()
    load_seg.wait()
    hw_row[...] = hw_ref[...].reshape(1, 8192).astype(F32)

    def squares(i, carry):
        total, dot = carry
        at = pl.ds(pl.multiple_of(i * 256, 256), 256)
        x = hid[:, at].astype(F32)
        return total + x * x, dot + x * hw_row[:, at]

    zero = jnp.zeros((128, 256), F32)
    total, dot = lax.fori_loop(0, 32, squares, (zero, zero))
    root = lax.rsqrt(jnp.sum(total, axis=1, keepdims=True) * (1.0 / 8192.0) + 1e-05)
    residual = jnp.sum(dot, axis=1, keepdims=True)
    my_rows = pl.ds(pl.multiple_of(core * 128, 128), 128)

    def normalise(i, _):
        at = pl.ds(pl.multiple_of(i * 256, 256), 256)
        normed = (hid[:, at].astype(F32) * root * gain_ref[:, at]).astype(BF)
        x3[i, my_rows, :] = nn(perm, normed).astype(BF)
        return 0

    lax.fori_loop(0, 32, normalise, 0)
    x_rows = x3.at[:, my_rows, :]
    x_copy = pltpu.make_async_remote_copy(
        src_ref=x_rows, dst_ref=x_rows, send_sem=xs_sem, recv_sem=xr_sem,
        device_id=(d, 2 * chip + 1 - core), device_id_type=MESH,
    )
    other_rows = x3.at[:, pl.ds(pl.multiple_of((1 - core) * 128, 128), 128), :]
    x_in = pltpu.make_async_remote_copy(
        src_ref=other_rows, dst_ref=other_rows, send_sem=xs_sem, recv_sem=xr_sem,
        device_id=(d, 2 * chip + 1 - core), device_id_type=MESH,
    )
    x_copy.start()
    weights[0].step2()
    weights[1].step1()
    weights[0].step3()
    weights[0].step4()

    def segment_keys(i, _):
        at = pl.ds(pl.multiple_of(i * 256, 256), 256)
        s = jnp.broadcast_to(seg_ref[:, at], (128, 256))
        k = iota((128, 256), 0)
        part = jnp.where((k < 8) & (s != k), NEG, 0.0)
        kext[i] = part.T.astype(BF)
        return 0

    lax.fori_loop(0, 16, segment_keys, 0)

    x_in.wait_recv()
    kacc[...] = jnp.zeros_like(kacc)
    vacc[...] = jnp.zeros_like(vacc)

    def project(g, par, du, dv):
        c = near(par, du, dv)
        x = x3[2 * c + par]
        base = pl.multiple_of(par * WROWS, 32)
        kacc[g] += nn(x, wg[g, c, pl.ds(base, 256), :])
        vacc[g] += nt(wg[g, c, pl.ds(base + 256, 16), :], x[:, 0:128]) + nt(
            wg[g, c, pl.ds(base + 272, 16), :], x[:, 128:256]
        )

    def project_all(g, places):
        for du, dv in places:
            def body(par, _, du=du, dv=dv):
                project(g, par, du, dv)
                return 0

            lax.fori_loop(0, 2, body, 0)

    def project_rest(g):
        for group, place_of in ((1, (0, 2)), (2, (-1, 2)), (3, (1, 2)), (4, (2, 2))):
            weights[g].step6(group)
            project_all(g, [place_of])

    def send_keys(g):
        k_rows = kacc[g].astype(BF)
        v = vacc[g]
        vf = v[0:8] + v[8:16]
        vf_hi = vf.astype(BF).astype(F32)
        v_rows = jnp.concatenate([vf_hi, vf - vf_hi, jnp.zeros((112, 256), F32)], axis=0)
        v_cols = v_rows.T.astype(BF)
        for s in range(2):
            for b in range(4):
                at = s * 128 + b * 32
                kvout[g, b, s, :, 0:128] = k_rows[at : at + 32]
                kvout[g, b, s, :, 128:256] = v_cols[at : at + 32]
        for dd in range(1, 4):
            k_copy(g, dd).start()
        kvin[g, d] = kvout[g, d]

    def take_keys(g):
        for dd in range(1, 4):
            k_arrival(g, dd).wait_recv()
        got_k = kvin[g, :, :, :, 0:128].reshape(256, 128)
        got_v = kvin[g, :, :, :, 128:256].reshape(256, 128).astype(F32).T[0:16].astype(BF)
        values = nn(got_v, onehot[...]).astype(BF)
        win[g, chip, 0:256, :] = nn(onehot_t[...], got_k).astype(BF)
        win[g, chip, 256:272, :] = values[:, 0:128]
        win[g, chip, 272:288, :] = values[:, 128:256]
        keys[g].begin()

    def k_copy(g, dd):
        b = (d + dd) % 4
        return pltpu.make_async_remote_copy(
            src_ref=kvout.at[g, b], dst_ref=kvin.at[g, d],
            send_sem=ks_sem.at[g, dd], recv_sem=kr_sem.at[g, dd],
            device_id=(b, f), device_id_type=MESH,
        )

    def k_arrival(g, dd):
        return pltpu.make_async_remote_copy(
            src_ref=kvout.at[g, d], dst_ref=kvin.at[g, (d - dd + 4) % 4],
            send_sem=ks_sem.at[g, dd], recv_sem=kr_sem.at[g, dd],
            device_id=((d + dd) % 4, f), device_id_type=MESH,
        )

    project_all(0, [(0, 0), (-1, 0), (1, 0), (0, -1), (0, 1), (2, 0)])
    weights[1].step2()
    weights[0].step5()
    weights[1].step3()
    project_all(0, [(-1, -1), (-1, 1), (1, -1), (1, 1), (2, -1), (2, 1)])
    weights[1].step4()
    project_rest(0)
    send_keys(0)
    weights[1].step5()
    project_all(1, [(0, 0), (-1, 0), (1, 0), (0, -1), (0, 1), (2, 0)])

    for dd, c in q_pairs:
        q_arrival(dd, c).wait_recv()
    off = qin[:, :, :, 2048:2176].reshape(256, 128).astype(F32)
    arrival = iota((256, 128), 0)
    place = off + ((arrival // 32) % 2).astype(F32) * 128.0
    place = jnp.concatenate([place, place], axis=1)
    hot = (place == iota((256, 256), 1).astype(F32)).astype(F32)
    onehot[...] = hot.astype(BF)
    onehot_t[...] = hot.T.astype(BF)
    take_keys(0)
    own_at = pl.ds(pl.multiple_of(chip * 256, 256), 256)
    seg_hot = (jnp.broadcast_to(seg_ref[:, own_at], (128, 256)) == iota((128, 256), 0)).astype(BF)
    qseg = nt(seg_hot, onehot[...]).astype(BF)
    later = jnp.where(iota((256, 256), 0) > iota((256, 256), 1), NEG, 0.0).astype(BF)
    bias[...] = nt(later, onehot[...])
    for h in range(16):
        qh = qin[:, :, :, h * 128 : (h + 1) * 128].reshape(256, 128)
        qx[h, 0:128, :] = qh.astype(F32).T.astype(BF)
        qx[h, 128:256, :] = qseg

    project_all(1, [(-1, -1), (-1, 1), (1, -1), (1, 1), (2, -1), (2, 1)])
    scale = LOG2E * 128.0 ** -0.5
    ones = jnp.ones((16, 256), BF)

    def attend(g, c, first):
        def scores(j):
            key = jnp.concatenate([win[g, c, 0:256, :], kext[c]], axis=1)
            s = nn(key, qx[g * 8 + j])
            sbuf[j] = s + bias[...] if first else s

        for j in range(4):
            scores(j)
        for batch in (0, 4):
            if batch == 0:
                for j in range(4, 8):
                    scores(j)
            for j in range(batch, batch + 4):
                h = g * 8 + j
                values = jnp.concatenate([win[g, c, 256:272, :], win[g, c, 272:288, :]], axis=1)
                val = jnp.concatenate([values, ones], axis=0)
                s = sbuf[j]
                new = jnp.max(s, axis=0, keepdims=True)
                if not first:
                    old = high[h]
                    new = jnp.maximum(old, new)
                p = jnp.exp2((s - new) * scale).astype(BF)
                part = nn(val, p)
                acc[h] = part if first else acc[h] * jnp.exp2((old - new) * scale) + part
                high[h] = new

    def attend_row(g, row):
        keys[g].row(row)

        def body(k, _):
            source = (y + k) % 4
            c = chip - y - 4 * row + source
            seen = (z >= row) & (c < chip) & (c >= chip - 8)

            @pl.when(seen)
            def _():
                attend(g, c, False)

            return 0

        lax.fori_loop(0, 4, body, 0)

    project_rest(1)
    send_keys(1)
    keys[0].forward()
    attend(0, chip, True)
    take_keys(1)
    attend_row(0, 0)
    keys[1].forward()
    attend_row(0, 1)
    attend_row(0, 2)
    attend(1, chip, True)
    for row in range(3):
        attend_row(1, row)

    branch = jnp.zeros((1, 256), F32)
    for h in range(16):
        a = acc[h]
        j = h % 8
        branch = branch + (a[j : j + 1] + a[8 + j : 9 + j]) / a[16:17]
    ret_out[...] = jnp.broadcast_to(branch, (8, 256))

    def r_copy(dd, c):
        n = dd * 2 + c
        return pltpu.make_async_remote_copy(
            src_ref=ret_out, dst_ref=ret_in.at[d, core],
            send_sem=rs_sem.at[n], recv_sem=rr_sem.at[n],
            device_id=((d + dd) % 4, 2 * chip + (core + c) % 2), device_id_type=MESH,
        )

    def r_arrival(dd, c):
        n = dd * 2 + c
        return pltpu.make_async_remote_copy(
            src_ref=ret_out, dst_ref=ret_in.at[(d - dd + 4) % 4, (core + c) % 2],
            send_sem=rs_sem.at[n], recv_sem=rr_sem.at[n],
            device_id=(d, 2 * chip + 1 - core), device_id_type=MESH,
        )

    for dd, c in q_pairs:
        r_copy(dd, c).start()
    ret_in[d, core] = ret_out[...]
    for dd, c in q_pairs:
        r_arrival(dd, c).wait_recv()

    lane = (d * 64 + core * 32).astype(F32) + rank_col
    lanes = iota((128, 256), 1).astype(F32)
    value = jnp.zeros((128, 256), F32)
    for b in range(4):
        row = ret_in[b, 0][0:1] + ret_in[b, 1][0:1]
        value = value + jnp.where((lanes == lane) & (bin_col == float(b)), row, 0.0)
    score = jnp.sum(value, axis=1, keepdims=True) + residual
    out_ref[...] = jnp.sum(jnp.where(eye, score, 0.0), axis=0, keepdims=True)

    x_copy.wait_send()
    for g in range(2):
        pair(g, core).wait_send()
        weights[g].finish()
        keys[g].finish()
    for dd, c in q_pairs:
        q_copy(dd, c).wait_send()
        r_copy(dd, c).wait_send()
    for g in range(2):
        for dd in range(1, 4):
            k_copy(g, dd).wait_send()


def on_device(
    hidden, queries, norm_gain, key_value_weight, head_weight, head_fold, route, segments
):
    vmem = pl.BlockSpec(memory_space=pltpu.VMEM)
    hbm = pl.BlockSpec(memory_space=pl.ANY)
    dma = pltpu.SemaphoreType.DMA
    out = pl.pallas_call(
        kernel,
        out_shape=jax.ShapeDtypeStruct((1, 128), F32),
        in_specs=[hbm] * 8,
        out_specs=vmem,
        scratch_shapes=[
            pltpu.VMEM((1, 8192), F32),
            pltpu.VMEM((8192,), BF),
            pltpu.VMEM((4096,), BF),
            pltpu.VMEM((2, 128), jnp.int32),
            pltpu.VMEM((1, 4096), jnp.int32),
            pltpu.VMEM((1, 8192), F32),
            pltpu.VMEM((128, 8192), BF),
            pltpu.VMEM((128, 4096), BF),
            pltpu.VMEM((256, 1024), BF),
            pltpu.VMEM((2, WROWS, 128), BF),
            pltpu.VMEM((32, 256, 256), BF),
            pltpu.VMEM((2, 16, 2 * WROWS, 128), BF),
            pltpu.VMEM((4, 2, 32, 2176), BF),
            pltpu.VMEM((4, 2, 32, 2176), BF),
            pltpu.VMEM((16, 256, 256), BF),
            pltpu.VMEM((2, 4, 2, 32, 256), BF),
            pltpu.VMEM((2, 4, 2, 32, 256), BF),
            pltpu.VMEM((2, 16, 2 * KROWS, 128), BF),
            pltpu.VMEM((16, 256, 128), BF),
            pltpu.VMEM((256, 256), F32),
            pltpu.VMEM((256, 256), BF),
            pltpu.VMEM((256, 256), BF),
            pltpu.VMEM((2, 256, 128), F32),
            pltpu.VMEM((2, 16, 256), F32),
            pltpu.VMEM((16, 1, 256), F32),
            pltpu.VMEM((16, 32, 256), F32),
            pltpu.VMEM((8, 256, 256), F32),
            pltpu.VMEM((8, 256), F32),
            pltpu.VMEM((4, 2, 8, 256), F32),
            dma((8,)),
            dma((2,)), dma((2,)), dma, dma,
            dma((8,)), dma((8,)),
            dma((2, 4)), dma((2, 4)),
            dma((8,)), dma((8,)),
            dma((2, 2, 5, 4)), dma((2, 2, 5, 4)),
            dma((2, 22)), dma((2, 22)),
        ],
        compiler_params=pltpu.CompilerParams(
            collective_id=0, has_side_effects=True, vmem_limit_bytes=62 * 1024 * 1024
        ),
        cost_estimate=pl.CostEstimate(
            flops=10_000_000_000, bytes_accessed=4_000_000, transcendentals=10_000_000
        ),
    )(
        hidden, queries, norm_gain.reshape(1, -1), key_value_weight,
        head_weight, head_fold, route, segments,
    )
    return out.reshape(-1)


def solution(mesh):
    in_specs = (
        P(("dp", "fsdp"), None),
        P(("dp", "fsdp"), None),
        P(),
        P("fsdp", None),
        P(),
        P(),
        P(None, ("dp", "fsdp")),
        P("dp", None),
    )
    out_specs = P(("dp", "fsdp"))
    return jax.shard_map(
        on_device, mesh=mesh, in_specs=in_specs, out_specs=out_specs, check_vma=False
    )
```

```python
import functools

import jax
import jax.numpy as jnp
from jax import lax
from jax.experimental import pallas as pl
from jax.experimental.pallas import tpu as pltpu
from jax.sharding import PartitionSpec as P

MESH = pl.DeviceIdType.MESH
BF = jnp.bfloat16
F32 = jnp.float32
LOG2E = 1.4426950408889634
NEG = -1e30
WROWS = (320, 256)
KROWS = 144


def nn(a, b):
    return lax.dot_general(a, b, (((1,), (0,)), ((), ())), preferred_element_type=F32)


def nt(a, b):
    return lax.dot_general(a, b, (((1,), (1,)), ((), ())), preferred_element_type=F32)


def iota(shape, axis):
    return lax.broadcasted_iota(jnp.int32, shape, axis)


def kernel(
    hid_hbm, q_hbm, gain_hbm, w_hbm, hw_hbm, fold_hbm, route_hbm, seg_hbm, out_ref,
    gain_ref, hw_ref, fold_ref, route_ref, seg_ref, hw_row, hid, qv, wv, wpair0, wpair1, x3, wg0, wg1, qout, qin, qx, kvout, kvin, win, kext, bias, onehot, onehot_t,
    kacc, vacc, high, acc, sbuf, ret_out, ret_in,
    load_sem, pair_send, pair_recv, xs_sem, xr_sem, qs_sem, qr_sem, ks_sem, kr_sem,
    rs_sem, rr_sem, ws_sem, wr_sem, gs_sem, gr_sem,
):
    d = lax.axis_index("dp")
    f = lax.axis_index("fsdp")
    chip = f // 2
    core = f % 2
    y = chip % 4
    z = chip // 4

    def chip_at(par, u, v):
        return (1 - par) * (4 * v + u) + par * (4 * u + v)

    def coords(par):
        return (1 - par) * y + par * z, (1 - par) * z + par * y

    def near(par, du, dv):
        u, v = coords(par)
        return chip_at(par, (u + du + 4) % 4, (v + dv + 4) % 4)

    barrier = pltpu.get_barrier_semaphore()
    peers = [(d, 2 * chip + (1 - core))]
    for dd in range(1, 4):
        for c in range(2):
            peers.append(((d + dd) % 4, 2 * chip + c))
    for du, dv in ((1, 0), (-1, 0), (0, 1), (0, -1), (2, 0), (0, 2)):
        peers.append((d, 2 * near(0, du, dv) + core))
    for peer in peers:
        pl.semaphore_signal(barrier, inc=1, device_id=peer, device_id_type=MESH)

    loads = [
        pltpu.make_async_copy(src, dst, load_sem.at[n])
        for n, (src, dst) in enumerate([
            (w_hbm, wv), (fold_hbm, fold_ref), (route_hbm, route_ref), (q_hbm, qv),
            (hid_hbm, hid), (hw_hbm, hw_ref), (gain_hbm, gain_ref), (seg_hbm, seg_ref),
        ])
    ]
    load_w, load_fold, load_route, load_q, load_h, load_hw, load_gain, load_seg = loads
    for load in loads:
        load.start()

    load_w.wait()
    load_fold.wait()
    fold = fold_ref[...].reshape(1, 4096).astype(F32)
    head_row = jnp.concatenate(
        [fold[:, h * 128 : (h + 1) * 128] for h in range(32)], axis=0
    )
    fold_t = jnp.concatenate([head_row] * 4, axis=1)
    fold_t = jnp.where(iota((32, 512), 0) // 8 == iota((32, 512), 1) // 128, fold_t, 0.0).astype(BF)
    wf = nt(fold_t, wv[:, 512:1024])
    wf_hi = wf.astype(BF).astype(F32)
    wf_lo = wf - wf_hi
    own_is_1 = core == 1

    def pick(a, b):
        return jnp.where(own_is_1, b, a), jnp.where(own_is_1, a, b)

    packs = []
    for c in range(2):
        rows = []
        for g in range(2):
            at = 16 * c + 8 * g
            rows += [wf_hi[at : at + 8], wf_lo[at : at + 8]]
        packs.append(jnp.concatenate(rows, axis=0).astype(BF))
    mine, theirs = pick(packs[0], packs[1])
    base = pl.multiple_of(core * WROWS[0], 32)
    for side in range(2):
        at = 256 + 32 * side
        wg0[chip, pl.ds(base + at, 32), :] = mine[:, side * 128 : (side + 1) * 128]
        wpair0[at : at + 32, :] = theirs[:, side * 128 : (side + 1) * 128]
    for g, (wg, wpair) in enumerate(((wg0, wpair0), (wg1, wpair1))):
        mine, theirs = pick(wv[:, g * 128 : g * 128 + 128], wv[:, g * 128 + 256 : g * 128 + 384])
        wg[chip, pl.ds(pl.multiple_of(core * WROWS[g], 32), 256), :] = mine
        wpair[0:256, :] = theirs

    pl.semaphore_wait(barrier, len(peers))

    def pair(g, side):
        at = pl.ds(pl.multiple_of(side * WROWS[g], 32), WROWS[g])
        return pltpu.make_async_remote_copy(
            src_ref=(wpair0, wpair1)[g], dst_ref=(wg0, wg1)[g].at[chip, at],
            send_sem=pair_send.at[g], recv_sem=pair_recv.at[g],
            device_id=(d, 2 * chip + 1 - core), device_id_type=MESH,
        )

    for g in range(2):
        pair(g, core).start()

    class Gather:
        def __init__(self, g):
            self.g, self.half, self.cut = g, WROWS[g], WROWS[g] // 2

        def part(self, par, kind):
            if kind < 2:
                off, n = 0, self.half
            elif kind == 2:
                off, n = 0, self.cut
            else:
                off, n = self.cut, self.half - self.cut
            return pl.ds(pl.multiple_of(par * self.half + off, 16), n)

        def copy(self, par, group, kind, incoming):
            step = 1 if kind in (0, 2) else -1
            hops = (1 if kind < 2 else 2) if incoming else (0 if kind < 2 else 1)
            back = -step * hops
            if group == 0:
                at = near(par, back, 0)
                to = near(par, step, 0)
            else:
                du = (0, -1, 1, 2)[group - 1]
                at = near(par, du, back)
                to = near(par, 0, step)
            ref = (wg0, wg1)[self.g].at[at, self.part(par, kind)]
            return pltpu.make_async_remote_copy(
                src_ref=ref, dst_ref=ref,
                send_sem=ws_sem.at[self.g, par, group, kind],
                recv_sem=wr_sem.at[self.g, par, group, kind],
                device_id=(d, 2 * to + core), device_id_type=MESH,
            )

        def send(self, par, group, kind):
            self.copy(par, group, kind, False).start()

        def wait(self, par, group, kind):
            self.copy(par, group, kind, True).wait_recv()

        def finish(self):
            for par in range(2):
                for group in range(5):
                    for kind in range(4):
                        self.copy(par, group, kind, False).wait_send()

        def begin(self, par, group):
            self.send(par, group, 0)
            self.send(par, group, 1)

        def step1(self):
            for kind in range(2):
                for par in range(2):
                    self.wait(par, 0, kind)
                    self.send(par, 2 + kind, 0)
                    self.send(par, 2 + kind, 1)
                    self.send(par, 0, 2 + kind)

        def step2(self):
            for kind in range(2):
                for par in range(2):
                    self.wait(par, 1, kind)
                    self.send(par, 1, 2 + kind)

        def step3(self):
            for par in range(2):
                self.wait(par, 0, 2)
                self.wait(par, 0, 3)
                self.send(par, 4, 0)
                self.send(par, 4, 1)

        def step4(self):
            for group in (2, 3):
                for kind in range(2):
                    for par in range(2):
                        self.wait(par, group, kind)
                        self.send(par, group, 2 + kind)

        def step5(self):
            for kind in range(2):
                for par in range(2):
                    self.wait(par, 4, kind)
                    self.send(par, 4, 2 + kind)

        def step6(self, group):
            for par in range(2):
                self.wait(par, group, 2)
                self.wait(par, group, 3)

    class Keys:
        def __init__(self, g):
            self.g = g

        def copy(self, n, at, par, to):
            ref = win.at[self.g, at, pl.ds(par * KROWS, KROWS)]
            return pltpu.make_async_remote_copy(
                src_ref=ref, dst_ref=ref,
                send_sem=gs_sem.at[self.g, n], recv_sem=gr_sem.at[self.g, n],
                device_id=(d, 2 * to + core), device_id_type=MESH,
            )

        def first_y(self, e, incoming):
            at = near(0, -e if incoming else 0, 0)
            return self.copy(e - 1, at, 0, near(0, e, 0)), True

        def first_z(self, j, incoming):
            at = near(0, 0, -j if incoming else 0)
            return self.copy(2 + j, at, 1, near(0, 0, j)), (z >= j if incoming else z < 4 - j)

        def then_z(self, k, j, incoming):
            at = near(0, k, -j if incoming else 0)
            ok = z >= j if incoming else z < 4 - j
            if j == 2:
                ok = ok & ((y + k) % 4 >= y)
            return self.copy(5 + 2 * k + j - 1, at, 0, near(0, 0, j)), ok

        def then_y(self, e, j, incoming):
            at = near(0, -e if incoming else 0, -j)
            source = (y - e + 4) % 4 if incoming else y
            target = y if incoming else (y + e) % 4
            ok = z >= j
            if j == 0:
                ok = source < target
            if j == 2:
                ok = ok & (source >= target)
            return self.copy(13 + 3 * j + e - 1, at, 1, near(0, e, 0)), ok

        def run(self, act, made):
            copy, ok = made
            if ok is True:
                act(copy)
            else:
                @pl.when(ok)
                def _():
                    act(copy)

        def send(self, kind, *which):
            self.run(lambda copy: copy.start(), kind(*which, False))

        def wait(self, kind, *which):
            self.run(lambda copy: copy.wait_recv(), kind(*which, True))

        def begin(self):
            for e in (1, 3, 2):
                self.send(self.first_y, e)
            for j in (1, 2):
                self.send(self.first_z, j)
            for j in (1, 2):
                self.send(self.then_z, 0, j)
            for e in (1, 3, 2):
                self.send(self.then_y, e, 0)

        def forward(self):
            self.wait(self.first_z, 1)
            for e in (1, 3, 2):
                self.send(self.then_y, e, 1)
            for e in (1, 3, 2):
                self.wait(self.first_y, e)
                for j in (1, 2):
                    self.send(self.then_z, (4 - e) % 4, j)
            self.wait(self.first_z, 2)
            for e in (1, 3, 2):
                self.send(self.then_y, e, 2)

        def row(self, j):
            for e in (1, 3, 2):
                self.wait(self.then_y, e, j)
            if j:
                for k in range(4):
                    self.wait(self.then_z, k, j)

        def finish(self):
            done = lambda copy: copy.wait_send()
            for e in (1, 2, 3):
                self.run(done, self.first_y(e, False))
                for j in range(3):
                    self.run(done, self.then_y(e, j, False))
            for j in (1, 2):
                self.run(done, self.first_z(j, False))
                for k in range(4):
                    self.run(done, self.then_z(k, j, False))

    weights = [Gather(0), Gather(1)]
    keys = [Keys(0), Keys(1)]

    for g in range(2):
        for group in range(2):
            if g == 0 or group == 0:
                weights[g].begin(core, group)
        pair(g, 1 - core).wait_recv()
        for group in range(2):
            if g == 0 or group == 0:
                weights[g].begin(1 - core, group)

    load_route.wait()
    route = route_ref[...]
    bins = jnp.broadcast_to(route[0:1, :], (128, 128))
    offs = jnp.broadcast_to(route[1:2, :], (128, 128))
    i0 = iota((128, 128), 0)
    i1 = iota((128, 128), 1)
    member = (bins == i0).astype(F32)
    before = (i0 < i1).astype(BF)
    count = nn(member.astype(BF), before)
    rank = jnp.sum(member * count, axis=0, keepdims=True)
    slot = route[0:1, :].astype(F32) * 32.0 + rank
    perm = (jnp.broadcast_to(slot, (128, 128)) == i0.astype(F32)).astype(BF)
    eye = i0 == i1
    off_col = jnp.sum(jnp.where(eye, offs.astype(F32), 0.0), axis=1, keepdims=True)
    bin_col = jnp.sum(jnp.where(eye, bins.astype(F32), 0.0), axis=1, keepdims=True)
    rank_col = jnp.sum(jnp.where(eye, jnp.broadcast_to(rank, (128, 128)), 0.0), axis=1, keepdims=True)

    load_q.wait()
    off_sorted = nn(perm, jnp.broadcast_to(off_col, (128, 128)).astype(BF)).astype(BF)
    for c in range(2):
        for b in range(4):
            qout[b, c, :, 2048:2176] = off_sorted[b * 32 : (b + 1) * 32]

    def sort_q(i, _):
        for c in range(2):
            src = pl.ds(pl.multiple_of(c * 2048 + i * 256, 256), 256)
            dst = pl.ds(pl.multiple_of(i * 256, 256), 256)
            block = nn(perm, qv[:, src]).astype(BF)
            for b in range(4):
                qout[b, c, :, dst] = block[b * 32 : (b + 1) * 32]
        return 0

    lax.fori_loop(0, 8, sort_q, 0)

    def q_copy(dd, c):
        b = (d + dd) % 4
        to = (core + c) % 2
        n = dd * 2 + c
        return pltpu.make_async_remote_copy(
            src_ref=qout.at[b, to], dst_ref=qin.at[d, core],
            send_sem=qs_sem.at[n], recv_sem=qr_sem.at[n],
            device_id=(b, 2 * chip + to), device_id_type=MESH,
        )

    def q_arrival(dd, c):
        n = dd * 2 + c
        return pltpu.make_async_remote_copy(
            src_ref=qout.at[d, core], dst_ref=qin.at[(d - dd + 4) % 4, (core + c) % 2],
            send_sem=qs_sem.at[n], recv_sem=qr_sem.at[n],
            device_id=(d, 2 * chip + 1 - core), device_id_type=MESH,
        )

    q_pairs = [(dd, c) for dd in range(4) for c in range(2) if dd or c]
    for dd, c in q_pairs:
        q_copy(dd, c).start()
    qin[d, core] = qout[d, core]

    weights[0].step1()
    for par in range(2):
        weights[1].begin(par, 1)

    load_h.wait()
    load_hw.wait()
    load_gain.wait()
    load_seg.wait()
    hw_row[...] = hw_ref[...].reshape(1, 8192).astype(F32)

    def squares(i, carry):
        total, dot = carry
        at = pl.ds(pl.multiple_of(i * 256, 256), 256)
        x = hid[:, at].astype(F32)
        return total + x * x, dot + x * hw_row[:, at]

    zero = jnp.zeros((128, 256), F32)
    total, dot = lax.fori_loop(0, 32, squares, (zero, zero))
    root = lax.rsqrt(jnp.sum(total, axis=1, keepdims=True) * (1.0 / 8192.0) + 1e-05)
    residual = jnp.sum(dot, axis=1, keepdims=True)
    my_rows = pl.ds(pl.multiple_of(core * 128, 128), 128)

    def normalise(i, _):
        at = pl.ds(pl.multiple_of(i * 256, 256), 256)
        normed = (hid[:, at].astype(F32) * root * gain_ref[:, at]).astype(BF)
        x3[i, my_rows, :] = nn(perm, normed).astype(BF)
        return 0

    lax.fori_loop(0, 32, normalise, 0)
    x_rows = x3.at[:, my_rows, :]
    x_copy = pltpu.make_async_remote_copy(
        src_ref=x_rows, dst_ref=x_rows, send_sem=xs_sem, recv_sem=xr_sem,
        device_id=(d, 2 * chip + 1 - core), device_id_type=MESH,
    )
    other_rows = x3.at[:, pl.ds(pl.multiple_of((1 - core) * 128, 128), 128), :]
    x_in = pltpu.make_async_remote_copy(
        src_ref=other_rows, dst_ref=other_rows, send_sem=xs_sem, recv_sem=xr_sem,
        device_id=(d, 2 * chip + 1 - core), device_id_type=MESH,
    )
    x_copy.start()
    weights[0].step2()
    weights[1].step1()
    weights[0].step3()
    weights[0].step4()

    def segment_keys(i, _):
        at = pl.ds(pl.multiple_of(i * 256, 256), 256)
        s = jnp.broadcast_to(seg_ref[:, at], (128, 256))
        k = iota((128, 256), 0)
        part = jnp.where((k < 8) & (s != k), NEG, 0.0)
        kext[i] = part.T.astype(BF)
        return 0

    lax.fori_loop(0, 16, segment_keys, 0)
    kext[16] = jnp.where(iota((256, 128), 1) < 8, NEG, 0.0).astype(BF)

    x_in.wait_recv()
    kacc[...] = jnp.zeros_like(kacc)
    vacc[...] = jnp.zeros_like(vacc)

    def project(g, places):
        wg = (wg0, wg1)[g]
        k_sum = kacc[g]
        v_sum = vacc[:, 0:32]
        for du, dv in places:
            for par in range(2):
                c = near(par, du, dv)
                x = x3[2 * c + par]
                base = par * WROWS[g]
                k_sum += nn(x, wg[c, base : base + 256, :])
                if g == 0:
                    folded = jnp.concatenate(
                        [wg[c, base + 256 : base + 288, :], wg[c, base + 288 : base + 320, :]], axis=1
                    )
                    v_sum += nt(x, folded)
        kacc[g] = k_sum
        if g == 0:
            vacc[:, 0:32] = v_sum

    def project_rest(g):
        for group, place_of in ((1, (0, 2)), (2, (-1, 2)), (3, (1, 2)), (4, (2, 2))):
            weights[g].step6(group)
            project(g, [place_of])

    def send_keys(g):
        k_rows = kacc[g].astype(BF)
        v = vacc[...].T[16 * g : 16 * g + 16]
        vf = v[0:8] + v[8:16]
        vf_hi = vf.astype(BF).astype(F32)
        v_rows = jnp.concatenate([vf_hi, vf - vf_hi, jnp.zeros((112, 256), F32)], axis=0)
        v_cols = v_rows.T.astype(BF)
        for s in range(2):
            for b in range(4):
                at = s * 128 + b * 32
                kvout[g, b, s, :, 0:128] = k_rows[at : at + 32]
                kvout[g, b, s, :, 128:256] = v_cols[at : at + 32]
        for dd in range(1, 4):
            k_copy(g, dd).start()
        kvin[g, d] = kvout[g, d]

    def take_keys(g):
        for dd in range(1, 4):
            k_arrival(g, dd).wait_recv()
        got_k = kvin[g, :, :, :, 0:128].reshape(256, 128)
        got_v = kvin[g, :, :, :, 128:256].reshape(256, 128).astype(F32).T[0:16].astype(BF)
        values = nn(got_v, onehot[...]).astype(BF)
        win[g, chip, 0:256, :] = nn(onehot_t[...], got_k).astype(BF)
        win[g, chip, 256:272, :] = values[:, 0:128]
        win[g, chip, 272:288, :] = values[:, 128:256]
        keys[g].begin()

    def k_copy(g, dd):
        b = (d + dd) % 4
        return pltpu.make_async_remote_copy(
            src_ref=kvout.at[g, b], dst_ref=kvin.at[g, d],
            send_sem=ks_sem.at[g, dd], recv_sem=kr_sem.at[g, dd],
            device_id=(b, f), device_id_type=MESH,
        )

    def k_arrival(g, dd):
        return pltpu.make_async_remote_copy(
            src_ref=kvout.at[g, d], dst_ref=kvin.at[g, (d - dd + 4) % 4],
            send_sem=ks_sem.at[g, dd], recv_sem=kr_sem.at[g, dd],
            device_id=((d + dd) % 4, f), device_id_type=MESH,
        )

    project(0, [(0, 0), (-1, 0), (1, 0)])
    weights[1].step2()
    weights[0].step5()
    weights[1].step3()
    project(0, [(0, -1), (0, 1), (2, 0)])
    weights[1].step4()
    project(0, [(-1, -1), (-1, 1), (1, -1)])
    project(0, [(1, 1), (2, -1), (2, 1)])
    project_rest(0)
    send_keys(0)
    weights[1].step5()
    project(1, [(0, 0), (-1, 0), (1, 0)])
    project(1, [(0, -1), (0, 1), (2, 0)])

    for dd, c in q_pairs:
        q_arrival(dd, c).wait_recv()
    off = qin[:, :, :, 2048:2176].reshape(256, 128).astype(F32)
    arrival = iota((256, 128), 0)
    place = off + ((arrival // 32) % 2).astype(F32) * 128.0
    place = jnp.concatenate([place, place], axis=1)
    hot = (place == iota((256, 256), 1).astype(F32)).astype(F32)
    onehot[...] = hot.astype(BF)
    onehot_t[...] = hot.T.astype(BF)
    take_keys(0)
    own_at = pl.ds(pl.multiple_of(chip * 256, 256), 256)
    seg_hot = (jnp.broadcast_to(seg_ref[:, own_at], (128, 256)) == iota((128, 256), 0)).astype(BF)
    qseg = nt(seg_hot, onehot[...]).astype(BF)
    later = jnp.where(iota((256, 256), 0) > iota((256, 256), 1), NEG, 0.0).astype(BF)
    bias[...] = nt(later, onehot[...])
    for h in range(16):
        qh = qin[:, :, :, h * 128 : (h + 1) * 128].reshape(256, 128)
        qx[h, 0:128, :] = qh.astype(F32).T.astype(BF)
        qx[h, 128:256, :] = qseg

    project(1, [(-1, -1), (-1, 1), (1, -1)])
    project(1, [(1, 1), (2, -1), (2, 1)])
    scale = LOG2E * 128.0 ** -0.5

    def attend(g, chunks, first):
        n = 256 * len(chunks)

        def scores(j):
            key = jnp.concatenate(
                [jnp.concatenate([win[g, c, 0:256, :], kext[e]], axis=1) for c, e in chunks], axis=0
            )
            s = nn(key, qx[g * 8 + j])
            sbuf[j, 0:n, :] = s + bias[...] if first else s

        for j in range(4):
            scores(j)
        for batch in (0, 4):
            if batch == 0:
                for j in range(4, 8):
                    scores(j)
            for j in range(batch, batch + 4):
                h = g * 8 + j
                values = [win[g, c, at : at + 16, :] for c, e in chunks for at in (256, 272)]
                val = jnp.concatenate([jnp.concatenate(values, axis=1), jnp.ones((16, n), BF)], axis=0)
                s = sbuf[j, 0:n, :]
                new = jnp.max(s, axis=0, keepdims=True)
                if not first:
                    old = high[h]
                    new = jnp.maximum(old, new)
                p = jnp.exp2((s - new) * scale).astype(BF)
                part = nn(val, p)
                acc[h] = part if first else acc[h] * jnp.exp2((old - new) * scale) + part
                high[h] = new

    def attend_pairs(g, ok, place):
        def body(i, _):
            attend(g, [place(2 * i), place(2 * i + 1)], False)
            return 0

        @pl.when(ok)
        def _():
            lax.fori_loop(0, 2, body, 0)

    def attend_middle(g):
        keys[g].row(1)
        first = chip - y - 4
        attend_pairs(g, z >= 1, lambda i: (first + i, first + i))

    def attend_ends(g):
        keys[g].row(0)
        keys[g].row(2)

        def place(i):
            later = (i + 4 - y) // 4
            seen = 1 - later * (1 - z // 2)
            c = chip - y + i - 8 * later
            return seen * c + (1 - seen) * chip, seen * c + (1 - seen) * 16

        attend_pairs(g, (z >= 2) | (y >= 1), place)

    project_rest(1)
    send_keys(1)
    keys[0].forward()
    attend(0, [(chip, chip)], True)
    take_keys(1)
    attend_middle(0)
    keys[1].forward()
    attend_ends(0)
    attend(1, [(chip, chip)], True)
    attend_middle(1)
    attend_ends(1)

    branch = jnp.zeros((1, 256), F32)
    for h in range(16):
        a = acc[h]
        j = h % 8
        branch = branch + (a[j : j + 1] + a[8 + j : 9 + j]) / a[16:17]
    ret_out[...] = jnp.broadcast_to(branch, (8, 256))

    def r_copy(dd, c):
        n = dd * 2 + c
        return pltpu.make_async_remote_copy(
            src_ref=ret_out, dst_ref=ret_in.at[d, core],
            send_sem=rs_sem.at[n], recv_sem=rr_sem.at[n],
            device_id=((d + dd) % 4, 2 * chip + (core + c) % 2), device_id_type=MESH,
        )

    def r_arrival(dd, c):
        n = dd * 2 + c
        return pltpu.make_async_remote_copy(
            src_ref=ret_out, dst_ref=ret_in.at[(d - dd + 4) % 4, (core + c) % 2],
            send_sem=rs_sem.at[n], recv_sem=rr_sem.at[n],
            device_id=(d, 2 * chip + 1 - core), device_id_type=MESH,
        )

    for dd, c in q_pairs:
        r_copy(dd, c).start()
    ret_in[d, core] = ret_out[...]
    for dd, c in q_pairs:
        r_arrival(dd, c).wait_recv()

    lane = (d * 64 + core * 32).astype(F32) + rank_col
    lanes = iota((128, 256), 1).astype(F32)
    value = jnp.zeros((128, 256), F32)
    for b in range(4):
        row = ret_in[b, 0][0:1] + ret_in[b, 1][0:1]
        value = value + jnp.where((lanes == lane) & (bin_col == float(b)), row, 0.0)
    score = jnp.sum(value, axis=1, keepdims=True) + residual
    out_ref[...] = jnp.sum(jnp.where(eye, score, 0.0), axis=0, keepdims=True)

    x_copy.wait_send()
    for g in range(2):
        pair(g, core).wait_send()
        weights[g].finish()
        keys[g].finish()
    for dd, c in q_pairs:
        q_copy(dd, c).wait_send()
        r_copy(dd, c).wait_send()
    for g in range(2):
        for dd in range(1, 4):
            k_copy(g, dd).wait_send()


def on_device(
    hidden, queries, norm_gain, key_value_weight, head_weight, head_fold, route, segments
):
    vmem = pl.BlockSpec(memory_space=pltpu.VMEM)
    hbm = pl.BlockSpec(memory_space=pl.ANY)
    dma = pltpu.SemaphoreType.DMA
    out = pl.pallas_call(
        kernel,
        out_shape=jax.ShapeDtypeStruct((1, 128), F32),
        in_specs=[hbm] * 8,
        out_specs=vmem,
        scratch_shapes=[
            pltpu.VMEM((1, 8192), F32),
            pltpu.VMEM((8192,), BF),
            pltpu.VMEM((4096,), BF),
            pltpu.VMEM((2, 128), jnp.int32),
            pltpu.VMEM((1, 4096), jnp.int32),
            pltpu.VMEM((1, 8192), F32),
            pltpu.VMEM((128, 8192), BF),
            pltpu.VMEM((128, 4096), BF),
            pltpu.VMEM((256, 1024), BF),
            pltpu.VMEM((WROWS[0], 128), BF),
            pltpu.VMEM((WROWS[1], 128), BF),
            pltpu.VMEM((32, 256, 256), BF),
            pltpu.VMEM((16, 2 * WROWS[0], 128), BF),
            pltpu.VMEM((16, 2 * WROWS[1], 128), BF),
            pltpu.VMEM((4, 2, 32, 2176), BF),
            pltpu.VMEM((4, 2, 32, 2176), BF),
            pltpu.VMEM((16, 256, 256), BF),
            pltpu.VMEM((2, 4, 2, 32, 256), BF),
            pltpu.VMEM((2, 4, 2, 32, 256), BF),
            pltpu.VMEM((2, 16, 2 * KROWS, 128), BF),
            pltpu.VMEM((17, 256, 128), BF),
            pltpu.VMEM((256, 256), F32),
            pltpu.VMEM((256, 256), BF),
            pltpu.VMEM((256, 256), BF),
            pltpu.VMEM((2, 256, 128), F32),
            pltpu.VMEM((256, 128), F32),
            pltpu.VMEM((16, 1, 256), F32),
            pltpu.VMEM((16, 32, 256), F32),
            pltpu.VMEM((8, 512, 256), F32),
            pltpu.VMEM((8, 256), F32),
            pltpu.VMEM((4, 2, 8, 256), F32),
            dma((8,)),
            dma((2,)), dma((2,)), dma, dma,
            dma((8,)), dma((8,)),
            dma((2, 4)), dma((2, 4)),
            dma((8,)), dma((8,)),
            dma((2, 2, 5, 4)), dma((2, 2, 5, 4)),
            dma((2, 22)), dma((2, 22)),
        ],
        compiler_params=pltpu.CompilerParams(
            collective_id=0, has_side_effects=True, vmem_limit_bytes=62 * 1024 * 1024
        ),
        cost_estimate=pl.CostEstimate(
            flops=10_000_000_000, bytes_accessed=4_000_000, transcendentals=10_000_000
        ),
    )(
        hidden, queries, norm_gain.reshape(1, -1), key_value_weight,
        head_weight, head_fold, route, segments,
    )
    return out.reshape(-1)


def solution(mesh):
    in_specs = (
        P(("dp", "fsdp"), None),
        P(("dp", "fsdp"), None),
        P(),
        P("fsdp", None),
        P(),
        P(),
        P(None, ("dp", "fsdp")),
        P("dp", None),
    )
    out_specs = P(("dp", "fsdp"))
    return jax.shard_map(
        on_device, mesh=mesh, in_specs=in_specs, out_specs=out_specs, check_vma=False
    )
```

```python
import functools

import jax
import jax.numpy as jnp
from jax import lax
from jax.experimental import pallas as pl
from jax.experimental.pallas import tpu as pltpu
from jax.sharding import PartitionSpec as P

MESH = pl.DeviceIdType.MESH
BF = jnp.bfloat16
F32 = jnp.float32
LOG2E = 1.4426950408889634
NEG = -1e30
WROWS = (288, 256)
KPART = ((0, 144), (144, 128))


def nn(a, b):
    return lax.dot_general(a, b, (((1,), (0,)), ((), ())), preferred_element_type=F32)


def nt(a, b):
    return lax.dot_general(a, b, (((1,), (1,)), ((), ())), preferred_element_type=F32)


def iota(shape, axis):
    return lax.broadcasted_iota(jnp.int32, shape, axis)


def kernel(
    hid_hbm, q_hbm, gain_hbm, w_hbm, hw_hbm, fold_hbm, route_hbm, seg_hbm, out_ref,
    gain_ref, hw_ref, fold_ref, route_ref, seg_ref, hw_row, hid, qv, wv, wpair0, wpair1, x3, wg0, wg1, qout, qin, qx, kvout, kvin, win, kext, bias, onehot, onehot_t,
    kacc, vacc, high, acc, sbuf, ret_out, ret_in,
    load_sem, pair_send, pair_recv, xs_sem, xr_sem, qs_sem, qr_sem, ks_sem, kr_sem,
    rs_sem, rr_sem, ws_sem, wr_sem, gs_sem, gr_sem,
):
    d = lax.axis_index("dp")
    f = lax.axis_index("fsdp")
    chip = f // 2
    core = f % 2
    y = chip % 4
    z = chip // 4

    def chip_at(par, u, v):
        return (1 - par) * (4 * v + u) + par * (4 * u + v)

    def coords(par):
        return (1 - par) * y + par * z, (1 - par) * z + par * y

    def near(par, du, dv):
        u, v = coords(par)
        return chip_at(par, (u + du + 4) % 4, (v + dv + 4) % 4)

    barrier = pltpu.get_barrier_semaphore()
    peers = [(d, 2 * chip + (1 - core))]
    for dd in range(1, 4):
        for c in range(2):
            peers.append(((d + dd) % 4, 2 * chip + c))
    for du, dv in ((1, 0), (-1, 0), (0, 1), (0, -1), (2, 0), (0, 2)):
        peers.append((d, 2 * near(0, du, dv) + core))
    for peer in peers:
        pl.semaphore_signal(barrier, inc=1, device_id=peer, device_id_type=MESH)

    loads = [
        pltpu.make_async_copy(src, dst, load_sem.at[n])
        for n, (src, dst) in enumerate([
            (w_hbm, wv), (fold_hbm, fold_ref), (route_hbm, route_ref), (q_hbm, qv),
            (hid_hbm, hid), (hw_hbm, hw_ref), (gain_hbm, gain_ref), (seg_hbm, seg_ref),
        ])
    ]
    load_w, load_fold, load_route, load_q, load_h, load_hw, load_gain, load_seg = loads
    for load in loads:
        load.start()

    load_w.wait()
    load_fold.wait()
    fold = fold_ref[...].reshape(1, 4096).astype(F32)
    head_row = jnp.concatenate(
        [fold[:, h * 128 : (h + 1) * 128] for h in range(32)], axis=0
    )
    fold_t = jnp.concatenate([head_row] * 4, axis=1)
    fold_t = jnp.where(iota((32, 512), 0) // 8 == iota((32, 512), 1) // 128, fold_t, 0.0).astype(BF)
    wf = nt(fold_t, wv[:, 512:1024])
    own_is_1 = core == 1

    def pick(a, b):
        return jnp.where(own_is_1, b, a), jnp.where(own_is_1, a, b)

    packs = [wf[16 * c : 16 * c + 16].astype(BF) for c in range(2)]
    mine, theirs = pick(packs[0], packs[1])
    base = pl.multiple_of(core * WROWS[0], 32)
    for side in range(2):
        at = 256 + 16 * side
        wg0[chip, pl.ds(base + at, 16), :] = mine[:, side * 128 : (side + 1) * 128]
        wpair0[at : at + 16, :] = theirs[:, side * 128 : (side + 1) * 128]
    for g, (wg, wpair) in enumerate(((wg0, wpair0), (wg1, wpair1))):
        mine, theirs = pick(wv[:, g * 128 : g * 128 + 128], wv[:, g * 128 + 256 : g * 128 + 384])
        wg[chip, pl.ds(pl.multiple_of(core * WROWS[g], 32), 256), :] = mine
        wpair[0:256, :] = theirs

    pl.semaphore_wait(barrier, len(peers))

    def pair(g, side):
        at = pl.ds(pl.multiple_of(side * WROWS[g], 32), WROWS[g])
        return pltpu.make_async_remote_copy(
            src_ref=(wpair0, wpair1)[g], dst_ref=(wg0, wg1)[g].at[chip, at],
            send_sem=pair_send.at[g], recv_sem=pair_recv.at[g],
            device_id=(d, 2 * chip + 1 - core), device_id_type=MESH,
        )

    for g in range(2):
        pair(g, core).start()

    class Gather:
        def __init__(self, g):
            self.g, self.half, self.cut = g, WROWS[g], WROWS[g] // 2

        def part(self, par, kind):
            if kind < 2:
                off, n = 0, self.half
            elif kind == 2:
                off, n = 0, self.cut
            else:
                off, n = self.cut, self.half - self.cut
            return pl.ds(pl.multiple_of(par * self.half + off, 16), n)

        def copy(self, par, group, kind, incoming):
            step = 1 if kind in (0, 2) else -1
            hops = (1 if kind < 2 else 2) if incoming else (0 if kind < 2 else 1)
            back = -step * hops
            if group == 0:
                at = near(par, back, 0)
                to = near(par, step, 0)
            else:
                du = (0, -1, 1, 2)[group - 1]
                at = near(par, du, back)
                to = near(par, 0, step)
            ref = (wg0, wg1)[self.g].at[at, self.part(par, kind)]
            return pltpu.make_async_remote_copy(
                src_ref=ref, dst_ref=ref,
                send_sem=ws_sem.at[self.g, par, group, kind],
                recv_sem=wr_sem.at[self.g, par, group, kind],
                device_id=(d, 2 * to + core), device_id_type=MESH,
            )

        def send(self, par, group, kind):
            self.copy(par, group, kind, False).start()

        def wait(self, par, group, kind):
            self.copy(par, group, kind, True).wait_recv()

        def finish(self):
            for par in range(2):
                for group in range(5):
                    for kind in range(4):
                        self.copy(par, group, kind, False).wait_send()

        def begin(self, par, group):
            self.send(par, group, 0)
            self.send(par, group, 1)

        def step1(self):
            for kind in range(2):
                for par in range(2):
                    self.wait(par, 0, kind)
                    self.send(par, 2 + kind, 0)
                    self.send(par, 2 + kind, 1)
                    self.send(par, 0, 2 + kind)

        def step2(self):
            for kind in range(2):
                for par in range(2):
                    self.wait(par, 1, kind)
                    self.send(par, 1, 2 + kind)

        def step3(self):
            for par in range(2):
                self.wait(par, 0, 2)
                self.wait(par, 0, 3)
                self.send(par, 4, 0)
                self.send(par, 4, 1)

        def step4(self):
            for group in (2, 3):
                for kind in range(2):
                    for par in range(2):
                        self.wait(par, group, kind)
                        self.send(par, group, 2 + kind)

        def step5(self):
            for kind in range(2):
                for par in range(2):
                    self.wait(par, 4, kind)
                    self.send(par, 4, 2 + kind)

        def step6(self, group):
            for par in range(2):
                self.wait(par, group, 2)
                self.wait(par, group, 3)

    class Keys:
        def __init__(self, g):
            self.g = g

        def copy(self, n, at, par, to):
            ref = win.at[self.g, at, pl.ds(*KPART[par])]
            return pltpu.make_async_remote_copy(
                src_ref=ref, dst_ref=ref,
                send_sem=gs_sem.at[self.g, n], recv_sem=gr_sem.at[self.g, n],
                device_id=(d, 2 * to + core), device_id_type=MESH,
            )

        def first_y(self, e, incoming):
            at = near(0, -e if incoming else 0, 0)
            return self.copy(e - 1, at, 0, near(0, e, 0)), True

        def first_z(self, j, incoming):
            at = near(0, 0, -j if incoming else 0)
            return self.copy(2 + j, at, 1, near(0, 0, j)), (z >= j if incoming else z < 4 - j)

        def then_z(self, k, j, incoming):
            at = near(0, k, -j if incoming else 0)
            ok = z >= j if incoming else z < 4 - j
            if j == 2:
                ok = ok & ((y + k) % 4 >= y)
            return self.copy(5 + 2 * k + j - 1, at, 0, near(0, 0, j)), ok

        def then_y(self, e, j, incoming):
            at = near(0, -e if incoming else 0, -j)
            source = (y - e + 4) % 4 if incoming else y
            target = y if incoming else (y + e) % 4
            ok = z >= j
            if j == 0:
                ok = source < target
            if j == 2:
                ok = ok & (source >= target)
            return self.copy(13 + 3 * j + e - 1, at, 1, near(0, e, 0)), ok

        def run(self, act, made):
            copy, ok = made
            if ok is True:
                act(copy)
            else:
                @pl.when(ok)
                def _():
                    act(copy)

        def send(self, kind, *which):
            self.run(lambda copy: copy.start(), kind(*which, False))

        def wait(self, kind, *which):
            self.run(lambda copy: copy.wait_recv(), kind(*which, True))

        def begin(self):
            for e in (1, 3, 2):
                self.send(self.first_y, e)
            for j in (1, 2):
                self.send(self.first_z, j)
            for j in (1, 2):
                self.send(self.then_z, 0, j)
            for e in (1, 3, 2):
                self.send(self.then_y, e, 0)

        def forward(self):
            self.wait(self.first_z, 1)
            for e in (1, 3, 2):
                self.send(self.then_y, e, 1)
            for e in (1, 3, 2):
                self.wait(self.first_y, e)
                for j in (1, 2):
                    self.send(self.then_z, (4 - e) % 4, j)
            self.wait(self.first_z, 2)
            for e in (1, 3, 2):
                self.send(self.then_y, e, 2)

        def row(self, j):
            for e in (1, 3, 2):
                self.wait(self.then_y, e, j)
            if j:
                for k in range(4):
                    self.wait(self.then_z, k, j)

        def finish(self):
            done = lambda copy: copy.wait_send()
            for e in (1, 2, 3):
                self.run(done, self.first_y(e, False))
                for j in range(3):
                    self.run(done, self.then_y(e, j, False))
            for j in (1, 2):
                self.run(done, self.first_z(j, False))
                for k in range(4):
                    self.run(done, self.then_z(k, j, False))

    weights = [Gather(0), Gather(1)]
    keys = [Keys(0), Keys(1)]

    for g in range(2):
        for group in range(2):
            if g == 0 or group == 0:
                weights[g].begin(core, group)
        pair(g, 1 - core).wait_recv()
        for group in range(2):
            if g == 0 or group == 0:
                weights[g].begin(1 - core, group)

    load_route.wait()
    route = route_ref[...]
    bins = jnp.broadcast_to(route[0:1, :], (128, 128))
    offs = jnp.broadcast_to(route[1:2, :], (128, 128))
    i0 = iota((128, 128), 0)
    i1 = iota((128, 128), 1)
    member = (bins == i0).astype(F32)
    before = (i0 < i1).astype(BF)
    count = nn(member.astype(BF), before)
    rank = jnp.sum(member * count, axis=0, keepdims=True)
    slot = route[0:1, :].astype(F32) * 32.0 + rank
    perm = (jnp.broadcast_to(slot, (128, 128)) == i0.astype(F32)).astype(BF)
    eye = i0 == i1
    off_col = jnp.sum(jnp.where(eye, offs.astype(F32), 0.0), axis=1, keepdims=True)
    bin_col = jnp.sum(jnp.where(eye, bins.astype(F32), 0.0), axis=1, keepdims=True)
    rank_col = jnp.sum(jnp.where(eye, jnp.broadcast_to(rank, (128, 128)), 0.0), axis=1, keepdims=True)

    load_q.wait()
    off_sorted = nn(perm, jnp.broadcast_to(off_col, (128, 128)).astype(BF)).astype(BF)
    for c in range(2):
        for b in range(4):
            qout[b, c, :, 2048:2176] = off_sorted[b * 32 : (b + 1) * 32]

    def sort_q(i, _):
        for c in range(2):
            src = pl.ds(pl.multiple_of(c * 2048 + i * 256, 256), 256)
            dst = pl.ds(pl.multiple_of(i * 256, 256), 256)
            block = nn(perm, qv[:, src]).astype(BF)
            for b in range(4):
                qout[b, c, :, dst] = block[b * 32 : (b + 1) * 32]
        return 0

    lax.fori_loop(0, 8, sort_q, 0)

    def q_copy(dd, c):
        b = (d + dd) % 4
        to = (core + c) % 2
        n = dd * 2 + c
        return pltpu.make_async_remote_copy(
            src_ref=qout.at[b, to], dst_ref=qin.at[d, core],
            send_sem=qs_sem.at[n], recv_sem=qr_sem.at[n],
            device_id=(b, 2 * chip + to), device_id_type=MESH,
        )

    def q_arrival(dd, c):
        n = dd * 2 + c
        return pltpu.make_async_remote_copy(
            src_ref=qout.at[d, core], dst_ref=qin.at[(d - dd + 4) % 4, (core + c) % 2],
            send_sem=qs_sem.at[n], recv_sem=qr_sem.at[n],
            device_id=(d, 2 * chip + 1 - core), device_id_type=MESH,
        )

    q_pairs = [(dd, c) for dd in range(4) for c in range(2) if dd or c]
    for dd, c in q_pairs:
        q_copy(dd, c).start()
    qin[d, core] = qout[d, core]

    weights[0].step1()
    for par in range(2):
        weights[1].begin(par, 1)

    load_h.wait()
    load_hw.wait()
    load_gain.wait()
    load_seg.wait()
    hw_row[...] = hw_ref[...].reshape(1, 8192).astype(F32)

    def squares(i, carry):
        total, dot = carry
        at = pl.ds(pl.multiple_of(i * 256, 256), 256)
        x = hid[:, at].astype(F32)
        return total + x * x, dot + x * hw_row[:, at]

    zero = jnp.zeros((128, 256), F32)
    total, dot = lax.fori_loop(0, 32, squares, (zero, zero))
    root = lax.rsqrt(jnp.sum(total, axis=1, keepdims=True) * (1.0 / 8192.0) + 1e-05)
    residual = jnp.sum(dot, axis=1, keepdims=True)
    weights[0].step2()
    weights[1].step1()
    my_rows = pl.ds(pl.multiple_of(core * 128, 128), 128)

    def normalise(i, _):
        at = pl.ds(pl.multiple_of(i * 256, 256), 256)
        normed = (hid[:, at].astype(F32) * root * gain_ref[:, at]).astype(BF)
        x3[i, my_rows, :] = nn(perm, normed).astype(BF)
        return 0

    lax.fori_loop(0, 32, normalise, 0)
    x_rows = x3.at[:, my_rows, :]
    x_copy = pltpu.make_async_remote_copy(
        src_ref=x_rows, dst_ref=x_rows, send_sem=xs_sem, recv_sem=xr_sem,
        device_id=(d, 2 * chip + 1 - core), device_id_type=MESH,
    )
    other_rows = x3.at[:, pl.ds(pl.multiple_of((1 - core) * 128, 128), 128), :]
    x_in = pltpu.make_async_remote_copy(
        src_ref=other_rows, dst_ref=other_rows, send_sem=xs_sem, recv_sem=xr_sem,
        device_id=(d, 2 * chip + 1 - core), device_id_type=MESH,
    )
    x_copy.start()
    weights[0].step3()
    weights[1].step2()
    weights[0].step4()

    def segment_keys(i, _):
        at = pl.ds(pl.multiple_of(i * 256, 256), 256)
        s = jnp.broadcast_to(seg_ref[:, at], (128, 256))
        k = iota((128, 256), 0)
        part = jnp.where((k < 8) & (s != k), NEG, 0.0)
        kext[i] = part.T.astype(BF)
        return 0

    lax.fori_loop(0, 16, segment_keys, 0)
    kext[16] = jnp.where(iota((256, 128), 1) < 8, NEG, 0.0).astype(BF)

    x_in.wait_recv()
    kacc[...] = jnp.zeros_like(kacc)
    vacc[...] = jnp.zeros_like(vacc)

    def project(g, places):
        wg = (wg0, wg1)[g]
        k_sum = kacc[g]
        v_sum = vacc[:, 0:16]
        for du, dv in places:
            for par in range(2):
                c = near(par, du, dv)
                x = x3[2 * c + par]
                base = par * WROWS[g]
                k_sum += nn(x, wg[c, base : base + 256, :])
                if g == 0:
                    folded = jnp.concatenate(
                        [wg[c, base + 256 : base + 272, :], wg[c, base + 272 : base + 288, :]], axis=1
                    )
                    v_sum += nt(x, folded)
        kacc[g] = k_sum
        if g == 0:
            vacc[:, 0:16] = v_sum

    def project_rest(g):
        for group, place_of in ((1, (0, 2)), (2, (-1, 2)), (3, (1, 2)), (4, (2, 2))):
            weights[g].step6(group)
            project(g, [place_of])

    def send_keys(g):
        k_rows = kacc[g].astype(BF)
        vf = vacc[...].T[8 * g : 8 * g + 8]
        v_rows = jnp.concatenate([vf, jnp.zeros((120, 256), F32)], axis=0)
        v_cols = v_rows.T.astype(BF)
        for s in range(2):
            for b in range(4):
                at = s * 128 + b * 32
                kvout[g, b, s, :, 0:128] = k_rows[at : at + 32]
                kvout[g, b, s, :, 128:256] = v_cols[at : at + 32]
        for dd in range(1, 4):
            k_copy(g, dd).start()
        kvin[g, d] = kvout[g, d]

    def take_keys(g):
        for dd in range(1, 4):
            k_arrival(g, dd).wait_recv()
        got_k = kvin[g, :, :, :, 0:128].reshape(256, 128)
        got_v = kvin[g, :, :, :, 128:256].reshape(256, 128).astype(F32).T[0:16].astype(BF)
        values = nn(got_v, onehot[...])[0:8]
        win[g, chip, 0:256, :] = nn(onehot_t[...], got_k).astype(BF)
        win[g, chip, 256:272, :] = jnp.concatenate([values[:, 0:128], values[:, 128:256]], axis=0).astype(BF)
        keys[g].begin()

    def k_copy(g, dd):
        b = (d + dd) % 4
        return pltpu.make_async_remote_copy(
            src_ref=kvout.at[g, b], dst_ref=kvin.at[g, d],
            send_sem=ks_sem.at[g, dd], recv_sem=kr_sem.at[g, dd],
            device_id=(b, f), device_id_type=MESH,
        )

    def k_arrival(g, dd):
        return pltpu.make_async_remote_copy(
            src_ref=kvout.at[g, d], dst_ref=kvin.at[g, (d - dd + 4) % 4],
            send_sem=ks_sem.at[g, dd], recv_sem=kr_sem.at[g, dd],
            device_id=((d + dd) % 4, f), device_id_type=MESH,
        )

    project(0, [(0, 0), (-1, 0), (1, 0)])
    weights[0].step5()
    weights[1].step3()
    project(0, [(0, -1), (0, 1), (2, 0)])
    weights[1].step4()
    project(0, [(-1, -1), (-1, 1), (1, -1)])
    project(0, [(1, 1), (2, -1), (2, 1)])
    project_rest(0)
    send_keys(0)
    weights[1].step5()
    project(1, [(0, 0), (-1, 0), (1, 0)])
    project(1, [(0, -1), (0, 1), (2, 0)])

    for dd, c in q_pairs:
        q_arrival(dd, c).wait_recv()
    off = qin[:, :, :, 2048:2176].reshape(256, 128).astype(F32)
    arrival = iota((256, 128), 0)
    place = off + ((arrival // 32) % 2).astype(F32) * 128.0
    place = jnp.concatenate([place, place], axis=1)
    hot = (place == iota((256, 256), 1).astype(F32)).astype(F32)
    onehot[...] = hot.astype(BF)
    onehot_t[...] = hot.T.astype(BF)
    take_keys(0)
    own_at = pl.ds(pl.multiple_of(chip * 256, 256), 256)
    seg_hot = (jnp.broadcast_to(seg_ref[:, own_at], (128, 256)) == iota((128, 256), 0)).astype(BF)
    qseg = nt(seg_hot, onehot[...]).astype(BF)
    later = jnp.where(iota((256, 256), 0) > iota((256, 256), 1), NEG, 0.0).astype(BF)
    bias[...] = nt(later, onehot[...])
    for h in range(16):
        qh = qin[:, :, :, h * 128 : (h + 1) * 128].reshape(256, 128)
        qx[h, 0:128, :] = qh.astype(F32).T.astype(BF)
        qx[h, 128:256, :] = qseg

    project(1, [(-1, -1), (-1, 1), (1, -1)])
    project(1, [(1, 1), (2, -1), (2, 1)])
    scale = LOG2E * 128.0 ** -0.5

    def attend(g, chunks, first):
        n = 256 * len(chunks)
        values = [win[g, c, 256:272, :].astype(F32) for c, e in chunks]
        values = jnp.concatenate([v[at : at + 8] for v in values for at in (0, 8)], axis=1)
        val = jnp.concatenate([values, jnp.ones((8, n), F32)], axis=0).astype(BF)

        def scores(j):
            key = jnp.concatenate(
                [jnp.concatenate([win[g, c, 0:256, :], kext[e]], axis=1) for c, e in chunks], axis=0
            )
            s = nn(key, qx[g * 8 + j])
            sbuf[j, 0:n, :] = s + bias[...] if first else s

        for j in range(4):
            scores(j)
        for batch in (0, 4):
            if batch == 0:
                for j in range(4, 8):
                    scores(j)
            for j in range(batch, batch + 4):
                h = g * 8 + j
                s = sbuf[j, 0:n, :]
                new = jnp.max(s, axis=0, keepdims=True)
                if not first:
                    old = high[h]
                    new = jnp.maximum(old, new)
                p = jnp.exp2((s - new) * scale).astype(BF)
                part = nn(val, p)
                acc[h] = part if first else acc[h] * jnp.exp2((old - new) * scale) + part
                high[h] = new

    def attend_pairs(g, ok, place):
        def body(i, _):
            attend(g, [place(2 * i), place(2 * i + 1)], False)
            return 0

        @pl.when(ok)
        def _():
            lax.fori_loop(0, 2, body, 0)

    def attend_middle(g):
        keys[g].row(1)
        first = chip - y - 4
        attend_pairs(g, z >= 1, lambda i: (first + i, first + i))

    def attend_ends(g):
        keys[g].row(0)
        keys[g].row(2)

        def place(i):
            later = (i + 4 - y) // 4
            seen = 1 - later * (1 - z // 2)
            c = chip - y + i - 8 * later
            return seen * c + (1 - seen) * chip, seen * c + (1 - seen) * 16

        attend_pairs(g, (z >= 2) | (y >= 1), place)

    project_rest(1)
    send_keys(1)
    keys[0].forward()
    attend(0, [(chip, chip)], True)
    take_keys(1)
    attend_middle(0)
    keys[1].forward()
    attend_ends(0)
    attend(1, [(chip, chip)], True)
    attend_middle(1)
    attend_ends(1)

    branch = jnp.zeros((1, 256), F32)
    for h in range(16):
        a = acc[h]
        j = h % 8
        branch = branch + a[j : j + 1] / a[8:9]
    ret_out[...] = jnp.broadcast_to(branch, (8, 256))

    def r_copy(dd, c):
        n = dd * 2 + c
        return pltpu.make_async_remote_copy(
            src_ref=ret_out, dst_ref=ret_in.at[d, core],
            send_sem=rs_sem.at[n], recv_sem=rr_sem.at[n],
            device_id=((d + dd) % 4, 2 * chip + (core + c) % 2), device_id_type=MESH,
        )

    def r_arrival(dd, c):
        n = dd * 2 + c
        return pltpu.make_async_remote_copy(
            src_ref=ret_out, dst_ref=ret_in.at[(d - dd + 4) % 4, (core + c) % 2],
            send_sem=rs_sem.at[n], recv_sem=rr_sem.at[n],
            device_id=(d, 2 * chip + 1 - core), device_id_type=MESH,
        )

    for dd, c in q_pairs:
        r_copy(dd, c).start()
    ret_in[d, core] = ret_out[...]
    for dd, c in q_pairs:
        r_arrival(dd, c).wait_recv()

    lane = (d * 64 + core * 32).astype(F32) + rank_col
    lanes = iota((128, 256), 1).astype(F32)
    value = jnp.zeros((128, 256), F32)
    for b in range(4):
        row = ret_in[b, 0][0:1] + ret_in[b, 1][0:1]
        value = value + jnp.where((lanes == lane) & (bin_col == float(b)), row, 0.0)
    score = jnp.sum(value, axis=1, keepdims=True) + residual
    out_ref[...] = jnp.sum(jnp.where(eye, score, 0.0), axis=0, keepdims=True)

    x_copy.wait_send()
    for g in range(2):
        pair(g, core).wait_send()
        weights[g].finish()
        keys[g].finish()
    for dd, c in q_pairs:
        q_copy(dd, c).wait_send()
        r_copy(dd, c).wait_send()
    for g in range(2):
        for dd in range(1, 4):
            k_copy(g, dd).wait_send()


def on_device(
    hidden, queries, norm_gain, key_value_weight, head_weight, head_fold, route, segments
):
    vmem = pl.BlockSpec(memory_space=pltpu.VMEM)
    hbm = pl.BlockSpec(memory_space=pl.ANY)
    dma = pltpu.SemaphoreType.DMA
    out = pl.pallas_call(
        kernel,
        out_shape=jax.ShapeDtypeStruct((1, 128), F32),
        in_specs=[hbm] * 8,
        out_specs=vmem,
        scratch_shapes=[
            pltpu.VMEM((1, 8192), F32),
            pltpu.VMEM((8192,), BF),
            pltpu.VMEM((4096,), BF),
            pltpu.VMEM((2, 128), jnp.int32),
            pltpu.VMEM((1, 4096), jnp.int32),
            pltpu.VMEM((1, 8192), F32),
            pltpu.VMEM((128, 8192), BF),
            pltpu.VMEM((128, 4096), BF),
            pltpu.VMEM((256, 1024), BF),
            pltpu.VMEM((WROWS[0], 128), BF),
            pltpu.VMEM((WROWS[1], 128), BF),
            pltpu.VMEM((32, 256, 256), BF),
            pltpu.VMEM((16, 2 * WROWS[0], 128), BF),
            pltpu.VMEM((16, 2 * WROWS[1], 128), BF),
            pltpu.VMEM((4, 2, 32, 2176), BF),
            pltpu.VMEM((4, 2, 32, 2176), BF),
            pltpu.VMEM((16, 256, 256), BF),
            pltpu.VMEM((2, 4, 2, 32, 256), BF),
            pltpu.VMEM((2, 4, 2, 32, 256), BF),
            pltpu.VMEM((2, 16, 272, 128), BF),
            pltpu.VMEM((17, 256, 128), BF),
            pltpu.VMEM((256, 256), F32),
            pltpu.VMEM((256, 256), BF),
            pltpu.VMEM((256, 256), BF),
            pltpu.VMEM((2, 256, 128), F32),
            pltpu.VMEM((256, 128), F32),
            pltpu.VMEM((16, 1, 256), F32),
            pltpu.VMEM((16, 16, 256), F32),
            pltpu.VMEM((8, 512, 256), F32),
            pltpu.VMEM((8, 256), F32),
            pltpu.VMEM((4, 2, 8, 256), F32),
            dma((8,)),
            dma((2,)), dma((2,)), dma, dma,
            dma((8,)), dma((8,)),
            dma((2, 4)), dma((2, 4)),
            dma((8,)), dma((8,)),
            dma((2, 2, 5, 4)), dma((2, 2, 5, 4)),
            dma((2, 22)), dma((2, 22)),
        ],
        compiler_params=pltpu.CompilerParams(
            collective_id=0, has_side_effects=True, vmem_limit_bytes=62 * 1024 * 1024
        ),
        cost_estimate=pl.CostEstimate(
            flops=10_000_000_000, bytes_accessed=4_000_000, transcendentals=10_000_000
        ),
    )(
        hidden, queries, norm_gain.reshape(1, -1), key_value_weight,
        head_weight, head_fold, route, segments,
    )
    return out.reshape(-1)


def solution(mesh):
    in_specs = (
        P(("dp", "fsdp"), None),
        P(("dp", "fsdp"), None),
        P(),
        P("fsdp", None),
        P(),
        P(),
        P(None, ("dp", "fsdp")),
        P("dp", None),
    )
    out_specs = P(("dp", "fsdp"))
    return jax.shard_map(
        on_device, mesh=mesh, in_specs=in_specs, out_specs=out_specs, check_vma=False
    )
```

```python
import functools

import jax
import jax.numpy as jnp
from jax import lax
from jax.experimental import pallas as pl
from jax.experimental.pallas import tpu as pltpu
from jax.sharding import PartitionSpec as P

MESH = pl.DeviceIdType.MESH
BF = jnp.bfloat16
F32 = jnp.float32
LOG2E = 1.4426950408889634
NEG = -1e30
WROWS = (288, 256)
KPART = ((0, 96), (96, 176))


def nn(a, b):
    return lax.dot_general(a, b, (((1,), (0,)), ((), ())), preferred_element_type=F32)


def nt(a, b):
    return lax.dot_general(a, b, (((1,), (1,)), ((), ())), preferred_element_type=F32)


def iota(shape, axis):
    return lax.broadcasted_iota(jnp.int32, shape, axis)


def kernel(
    hid_hbm, q_hbm, gain_hbm, w_hbm, hw_hbm, fold_hbm, route_hbm, seg_hbm, out_ref,
    gain_ref, hw_ref, fold_ref, route_ref, seg_ref, hw_row, hid, qv, wv, wpair0, wpair1, x3, wg0, wg1, qout, qin, qx, kvout, kvin, win, kext, bias, onehot, onehot_t,
    kacc, vacc, high, acc, sbuf, ret_out, ret_in,
    load_sem, pair_send, pair_recv, xs_sem, xr_sem, qs_sem, qr_sem, ks_sem, kr_sem,
    rs_sem, rr_sem, ws_sem, wr_sem, gs_sem, gr_sem,
):
    d = lax.axis_index("dp")
    f = lax.axis_index("fsdp")
    chip = f // 2
    core = f % 2
    y = chip % 4
    z = chip // 4

    def chip_at(par, u, v):
        return (1 - par) * (4 * v + u) + par * (4 * u + v)

    def coords(par):
        return (1 - par) * y + par * z, (1 - par) * z + par * y

    def near(par, du, dv):
        u, v = coords(par)
        return chip_at(par, (u + du + 4) % 4, (v + dv + 4) % 4)

    barrier = pltpu.get_barrier_semaphore()
    peers = [(d, 2 * chip + (1 - core))]
    for dd in range(1, 4):
        for c in range(2):
            peers.append(((d + dd) % 4, 2 * chip + c))
    for du, dv in ((1, 0), (-1, 0), (0, 1), (0, -1), (2, 0), (0, 2)):
        peers.append((d, 2 * near(0, du, dv) + core))
    for peer in peers:
        pl.semaphore_signal(barrier, inc=1, device_id=peer, device_id_type=MESH)

    loads = [
        pltpu.make_async_copy(src, dst, load_sem.at[n])
        for n, (src, dst) in enumerate([
            (w_hbm, wv), (fold_hbm, fold_ref), (route_hbm, route_ref), (q_hbm, qv),
            (hid_hbm, hid), (hw_hbm, hw_ref), (gain_hbm, gain_ref), (seg_hbm, seg_ref),
        ])
    ]
    load_w, load_fold, load_route, load_q, load_h, load_hw, load_gain, load_seg = loads
    for load in loads:
        load.start()

    load_w.wait()
    load_fold.wait()
    fold = fold_ref[...].reshape(1, 4096).astype(F32)
    head_row = jnp.concatenate(
        [fold[:, h * 128 : (h + 1) * 128] for h in range(32)], axis=0
    )
    fold_t = jnp.concatenate([head_row] * 4, axis=1)
    fold_t = jnp.where(iota((32, 512), 0) // 8 == iota((32, 512), 1) // 128, fold_t, 0.0).astype(BF)
    wf = nt(fold_t, wv[:, 512:1024])
    own_is_1 = core == 1

    def pick(a, b):
        return jnp.where(own_is_1, b, a), jnp.where(own_is_1, a, b)

    packs = [wf[16 * c : 16 * c + 16].astype(BF) for c in range(2)]
    mine, theirs = pick(packs[0], packs[1])
    base = pl.multiple_of(core * WROWS[0], 32)
    for side in range(2):
        at = 256 + 16 * side
        wg0[chip, pl.ds(base + at, 16), :] = mine[:, side * 128 : (side + 1) * 128]
        wpair0[at : at + 16, :] = theirs[:, side * 128 : (side + 1) * 128]
    for g, (wg, wpair) in enumerate(((wg0, wpair0), (wg1, wpair1))):
        mine, theirs = pick(wv[:, g * 128 : g * 128 + 128], wv[:, g * 128 + 256 : g * 128 + 384])
        wg[chip, pl.ds(pl.multiple_of(core * WROWS[g], 32), 256), :] = mine
        wpair[0:256, :] = theirs

    pl.semaphore_wait(barrier, len(peers))

    def pair(g, side):
        at = pl.ds(pl.multiple_of(side * WROWS[g], 32), WROWS[g])
        return pltpu.make_async_remote_copy(
            src_ref=(wpair0, wpair1)[g], dst_ref=(wg0, wg1)[g].at[chip, at],
            send_sem=pair_send.at[g], recv_sem=pair_recv.at[g],
            device_id=(d, 2 * chip + 1 - core), device_id_type=MESH,
        )

    for g in range(2):
        pair(g, core).start()

    class Gather:
        def __init__(self, g):
            self.g, self.half, self.cut = g, WROWS[g], WROWS[g] // 2

        def part(self, par, kind):
            if kind < 2:
                off, n = 0, self.half
            elif kind == 2:
                off, n = 0, self.cut
            else:
                off, n = self.cut, self.half - self.cut
            return pl.ds(pl.multiple_of(par * self.half + off, 16), n)

        def copy(self, par, group, kind, incoming):
            step = 1 if kind in (0, 2) else -1
            hops = (1 if kind < 2 else 2) if incoming else (0 if kind < 2 else 1)
            back = -step * hops
            if group == 0:
                at = near(par, back, 0)
                to = near(par, step, 0)
            else:
                du = (0, -1, 1, 2)[group - 1]
                at = near(par, du, back)
                to = near(par, 0, step)
            ref = (wg0, wg1)[self.g].at[at, self.part(par, kind)]
            return pltpu.make_async_remote_copy(
                src_ref=ref, dst_ref=ref,
                send_sem=ws_sem.at[self.g, par, group, kind],
                recv_sem=wr_sem.at[self.g, par, group, kind],
                device_id=(d, 2 * to + core), device_id_type=MESH,
            )

        def send(self, par, group, kind):
            self.copy(par, group, kind, False).start()

        def wait(self, par, group, kind):
            self.copy(par, group, kind, True).wait_recv()

        def finish(self):
            for par in range(2):
                for group in range(5):
                    for kind in range(4):
                        self.copy(par, group, kind, False).wait_send()

        def begin(self, par, group):
            self.send(par, group, 0)
            self.send(par, group, 1)

        def step1(self):
            for kind in range(2):
                for par in range(2):
                    self.wait(par, 0, kind)
                    self.send(par, 2 + kind, 0)
                    self.send(par, 2 + kind, 1)
                    self.send(par, 0, 2 + kind)

        def step2(self):
            for kind in range(2):
                for par in range(2):
                    self.wait(par, 1, kind)
                    self.send(par, 1, 2 + kind)

        def step3(self):
            for par in range(2):
                self.wait(par, 0, 2)
                self.wait(par, 0, 3)
                self.send(par, 4, 0)
                self.send(par, 4, 1)

        def step4(self):
            for group in (2, 3):
                for kind in range(2):
                    for par in range(2):
                        self.wait(par, group, kind)
                        self.send(par, group, 2 + kind)

        def step5(self):
            for kind in range(2):
                for par in range(2):
                    self.wait(par, 4, kind)
                    self.send(par, 4, 2 + kind)

        def step6(self, group):
            for par in range(2):
                self.wait(par, group, 2)
                self.wait(par, group, 3)

    class Keys:
        def __init__(self, g):
            self.g = g

        def copy(self, n, at, par, to):
            ref = win.at[self.g, at, pl.ds(*KPART[par])]
            return pltpu.make_async_remote_copy(
                src_ref=ref, dst_ref=ref,
                send_sem=gs_sem.at[self.g, n], recv_sem=gr_sem.at[self.g, n],
                device_id=(d, 2 * to + core), device_id_type=MESH,
            )

        def first_y(self, e, incoming):
            at = near(0, -e if incoming else 0, 0)
            return self.copy(e - 1, at, 0, near(0, e, 0)), True

        def first_z(self, j, incoming):
            at = near(0, 0, -j if incoming else 0)
            return self.copy(2 + j, at, 1, near(0, 0, j)), (z >= j if incoming else z < 4 - j)

        def then_z(self, k, j, incoming):
            at = near(0, k, -j if incoming else 0)
            ok = z >= j if incoming else z < 4 - j
            if j == 2:
                ok = ok & ((y + k) % 4 >= y)
            return self.copy(5 + 2 * k + j - 1, at, 0, near(0, 0, j)), ok

        def then_y(self, e, j, incoming):
            at = near(0, -e if incoming else 0, -j)
            source = (y - e + 4) % 4 if incoming else y
            target = y if incoming else (y + e) % 4
            ok = z >= j
            if j == 0:
                ok = source < target
            if j == 2:
                ok = ok & (source >= target)
            return self.copy(13 + 3 * j + e - 1, at, 1, near(0, e, 0)), ok

        def run(self, act, made):
            copy, ok = made
            if ok is True:
                act(copy)
            else:
                @pl.when(ok)
                def _():
                    act(copy)

        def send(self, kind, *which):
            self.run(lambda copy: copy.start(), kind(*which, False))

        def wait(self, kind, *which):
            self.run(lambda copy: copy.wait_recv(), kind(*which, True))

        def begin(self):
            for e in (1, 3, 2):
                self.send(self.first_y, e)
            self.send(self.first_z, 1)
            self.send(self.then_z, 0, 1)
            for e in (1, 3, 2):
                self.send(self.then_y, e, 0)
            self.send(self.first_z, 2)
            self.send(self.then_z, 0, 2)

        def forward(self):
            self.wait(self.first_z, 1)
            for e in (1, 3, 2):
                self.send(self.then_y, e, 1)
            for e in (1, 3, 2):
                self.wait(self.first_y, e)
                self.send(self.then_z, 4 - e, 1)
            for e in (1, 3, 2):
                self.send(self.then_z, 4 - e, 2)
            self.wait(self.first_z, 2)
            for e in (1, 3, 2):
                self.send(self.then_y, e, 2)

        def row(self, j):
            for e in (1, 3, 2):
                self.wait(self.then_y, e, j)
            if j:
                for k in range(4):
                    self.wait(self.then_z, k, j)

        def finish(self):
            done = lambda copy: copy.wait_send()
            for e in (1, 2, 3):
                self.run(done, self.first_y(e, False))
                for j in range(3):
                    self.run(done, self.then_y(e, j, False))
            for j in (1, 2):
                self.run(done, self.first_z(j, False))
                for k in range(4):
                    self.run(done, self.then_z(k, j, False))

    weights = [Gather(0), Gather(1)]
    keys = [Keys(0), Keys(1)]

    for g in range(2):
        for group in range(2):
            if g == 0 or group == 0:
                weights[g].begin(core, group)
        pair(g, 1 - core).wait_recv()
        for group in range(2):
            if g == 0 or group == 0:
                weights[g].begin(1 - core, group)

    load_route.wait()
    route = route_ref[...]
    bins = jnp.broadcast_to(route[0:1, :], (128, 128))
    offs = jnp.broadcast_to(route[1:2, :], (128, 128))
    i0 = iota((128, 128), 0)
    i1 = iota((128, 128), 1)
    member = (bins == i0).astype(F32)
    before = (i0 < i1).astype(BF)
    count = nn(member.astype(BF), before)
    rank = jnp.sum(member * count, axis=0, keepdims=True)
    slot = route[0:1, :].astype(F32) * 32.0 + rank
    perm = (jnp.broadcast_to(slot, (128, 128)) == i0.astype(F32)).astype(BF)
    eye = i0 == i1
    off_col = jnp.sum(jnp.where(eye, offs.astype(F32), 0.0), axis=1, keepdims=True)
    bin_col = jnp.sum(jnp.where(eye, bins.astype(F32), 0.0), axis=1, keepdims=True)
    rank_col = jnp.sum(jnp.where(eye, jnp.broadcast_to(rank, (128, 128)), 0.0), axis=1, keepdims=True)

    load_q.wait()
    off_sorted = nn(perm, jnp.broadcast_to(off_col, (128, 128)).astype(BF)).astype(BF)
    for c in range(2):
        for b in range(4):
            qout[b, c, :, 2048:2176] = off_sorted[b * 32 : (b + 1) * 32]

    def sort_q(i, _):
        for c in range(2):
            src = pl.ds(pl.multiple_of(c * 2048 + i * 256, 256), 256)
            dst = pl.ds(pl.multiple_of(i * 256, 256), 256)
            block = nn(perm, qv[:, src]).astype(BF)
            for b in range(4):
                qout[b, c, :, dst] = block[b * 32 : (b + 1) * 32]
        return 0

    lax.fori_loop(0, 8, sort_q, 0)

    def q_copy(dd, c):
        b = (d + dd) % 4
        to = (core + c) % 2
        n = dd * 2 + c
        return pltpu.make_async_remote_copy(
            src_ref=qout.at[b, to], dst_ref=qin.at[d, core],
            send_sem=qs_sem.at[n], recv_sem=qr_sem.at[n],
            device_id=(b, 2 * chip + to), device_id_type=MESH,
        )

    def q_arrival(dd, c):
        n = dd * 2 + c
        return pltpu.make_async_remote_copy(
            src_ref=qout.at[d, core], dst_ref=qin.at[(d - dd + 4) % 4, (core + c) % 2],
            send_sem=qs_sem.at[n], recv_sem=qr_sem.at[n],
            device_id=(d, 2 * chip + 1 - core), device_id_type=MESH,
        )

    q_pairs = [(dd, c) for dd in range(4) for c in range(2) if dd or c]
    for dd, c in q_pairs:
        q_copy(dd, c).start()
    qin[d, core] = qout[d, core]

    weights[0].step1()
    for par in range(2):
        weights[1].begin(par, 1)

    load_h.wait()
    load_hw.wait()
    load_gain.wait()
    load_seg.wait()
    hw_row[...] = hw_ref[...].reshape(1, 8192).astype(F32)

    def squares(i, carry):
        total, dot = carry
        at = pl.ds(pl.multiple_of(i * 256, 256), 256)
        x = hid[:, at].astype(F32)
        return total + x * x, dot + x * hw_row[:, at]

    zero = jnp.zeros((128, 256), F32)
    total, dot = lax.fori_loop(0, 32, squares, (zero, zero))
    root = lax.rsqrt(jnp.sum(total, axis=1, keepdims=True) * (1.0 / 8192.0) + 1e-05)
    residual = jnp.sum(dot, axis=1, keepdims=True)
    weights[0].step2()
    weights[1].step1()
    my_rows = pl.ds(pl.multiple_of(core * 128, 128), 128)

    def normalise(i, _):
        at = pl.ds(pl.multiple_of(i * 256, 256), 256)
        normed = (hid[:, at].astype(F32) * root * gain_ref[:, at]).astype(BF)
        x3[i, my_rows, :] = nn(perm, normed).astype(BF)
        return 0

    lax.fori_loop(0, 32, normalise, 0)
    x_rows = x3.at[:, my_rows, :]
    x_copy = pltpu.make_async_remote_copy(
        src_ref=x_rows, dst_ref=x_rows, send_sem=xs_sem, recv_sem=xr_sem,
        device_id=(d, 2 * chip + 1 - core), device_id_type=MESH,
    )
    other_rows = x3.at[:, pl.ds(pl.multiple_of((1 - core) * 128, 128), 128), :]
    x_in = pltpu.make_async_remote_copy(
        src_ref=other_rows, dst_ref=other_rows, send_sem=xs_sem, recv_sem=xr_sem,
        device_id=(d, 2 * chip + 1 - core), device_id_type=MESH,
    )
    x_copy.start()
    weights[0].step3()
    weights[1].step2()
    weights[0].step4()

    def segment_keys(i, _):
        at = pl.ds(pl.multiple_of(i * 256, 256), 256)
        s = jnp.broadcast_to(seg_ref[:, at], (128, 256))
        k = iota((128, 256), 0)
        part = jnp.where((k < 8) & (s != k), NEG, 0.0)
        kext[i] = part.T.astype(BF)
        return 0

    lax.fori_loop(0, 16, segment_keys, 0)
    kext[16] = jnp.where(iota((256, 128), 1) < 8, NEG, 0.0).astype(BF)

    x_in.wait_recv()
    kacc[...] = jnp.zeros_like(kacc)
    vacc[...] = jnp.zeros_like(vacc)

    def project(g, places):
        wg = (wg0, wg1)[g]
        k_sum = kacc[g]
        v_sum = vacc[:, 0:16]
        for du, dv in places:
            for par in range(2):
                c = near(par, du, dv)
                x = x3[2 * c + par]
                base = par * WROWS[g]
                k_sum += nn(x, wg[c, base : base + 256, :])
                if g == 0:
                    folded = jnp.concatenate(
                        [wg[c, base + 256 : base + 272, :], wg[c, base + 272 : base + 288, :]], axis=1
                    )
                    v_sum += nt(x, folded)
        kacc[g] = k_sum
        if g == 0:
            vacc[:, 0:16] = v_sum

    def project_rest(g):
        for group, place_of in ((1, (0, 2)), (2, (-1, 2)), (3, (1, 2)), (4, (2, 2))):
            weights[g].step6(group)
            project(g, [place_of])

    def send_keys(g):
        k_rows = kacc[g].astype(BF)
        vf = vacc[...].T[8 * g : 8 * g + 8]
        v_rows = jnp.concatenate([vf, jnp.zeros((120, 256), F32)], axis=0)
        v_cols = v_rows.T.astype(BF)
        for s in range(2):
            for b in range(4):
                at = s * 128 + b * 32
                kvout[g, b, s, :, 0:128] = k_rows[at : at + 32]
                kvout[g, b, s, :, 128:256] = v_cols[at : at + 32]
        for dd in range(1, 4):
            k_copy(g, dd).start()
        kvin[g, d] = kvout[g, d]

    def take_keys(g):
        for dd in range(1, 4):
            k_arrival(g, dd).wait_recv()
        got_k = kvin[g, :, :, :, 0:128].reshape(256, 128)
        got_v = kvin[g, :, :, :, 128:256].reshape(256, 128).astype(F32).T[0:16].astype(BF)
        values = nn(got_v, onehot[...])[0:8]
        win[g, chip, 0:256, :] = nn(onehot_t[...], got_k).astype(BF)
        win[g, chip, 256:272, :] = jnp.concatenate([values[:, 0:128], values[:, 128:256]], axis=0).astype(BF)
        keys[g].begin()

    def k_copy(g, dd):
        b = (d + dd) % 4
        return pltpu.make_async_remote_copy(
            src_ref=kvout.at[g, b], dst_ref=kvin.at[g, d],
            send_sem=ks_sem.at[g, dd], recv_sem=kr_sem.at[g, dd],
            device_id=(b, f), device_id_type=MESH,
        )

    def k_arrival(g, dd):
        return pltpu.make_async_remote_copy(
            src_ref=kvout.at[g, d], dst_ref=kvin.at[g, (d - dd + 4) % 4],
            send_sem=ks_sem.at[g, dd], recv_sem=kr_sem.at[g, dd],
            device_id=((d + dd) % 4, f), device_id_type=MESH,
        )

    project(0, [(0, 0), (-1, 0), (1, 0)])
    weights[0].step5()
    weights[1].step3()
    project(0, [(0, -1), (0, 1), (2, 0)])
    weights[1].step4()
    project(0, [(-1, -1), (-1, 1), (1, -1)])
    project(0, [(1, 1), (2, -1), (2, 1)])
    project_rest(0)
    send_keys(0)
    weights[1].step5()
    project(1, [(0, 0), (-1, 0), (1, 0)])
    project(1, [(0, -1), (0, 1), (2, 0)])

    for dd, c in q_pairs:
        q_arrival(dd, c).wait_recv()
    off = qin[:, :, :, 2048:2176].reshape(256, 128).astype(F32)
    arrival = iota((256, 128), 0)
    place = off + ((arrival // 32) % 2).astype(F32) * 128.0
    place = jnp.concatenate([place, place], axis=1)
    hot = (place == iota((256, 256), 1).astype(F32)).astype(F32)
    onehot[...] = hot.astype(BF)
    onehot_t[...] = hot.T.astype(BF)
    take_keys(0)
    own_at = pl.ds(pl.multiple_of(chip * 256, 256), 256)
    seg_hot = (jnp.broadcast_to(seg_ref[:, own_at], (128, 256)) == iota((128, 256), 0)).astype(BF)
    qseg = nt(seg_hot, onehot[...]).astype(BF)
    later = jnp.where(iota((256, 256), 0) > iota((256, 256), 1), NEG, 0.0).astype(BF)
    bias[...] = nt(later, onehot[...])
    for h in range(16):
        qh = qin[:, :, :, h * 128 : (h + 1) * 128].reshape(256, 128)
        qx[h, 0:128, :] = qh.astype(F32).T.astype(BF)
        qx[h, 128:256, :] = qseg

    project(1, [(-1, -1), (-1, 1), (1, -1)])
    project(1, [(1, 1), (2, -1), (2, 1)])
    scale = LOG2E * 128.0 ** -0.5

    def attend(g, chunks, first):
        n = 256 * len(chunks)
        values = [win[g, c, 256:272, :].astype(F32) for c, e in chunks]
        values = jnp.concatenate([v[at : at + 8] for v in values for at in (0, 8)], axis=1)
        val = jnp.concatenate([values, jnp.ones((8, n), F32)], axis=0).astype(BF)

        def scores(j):
            key = jnp.concatenate(
                [jnp.concatenate([win[g, c, 0:256, :], kext[e]], axis=1) for c, e in chunks], axis=0
            )
            s = nn(key, qx[g * 8 + j])
            sbuf[j, 0:n, :] = s + bias[...] if first else s

        for j in range(4):
            scores(j)
        for batch in (0, 4):
            if batch == 0:
                for j in range(4, 8):
                    scores(j)
            for j in range(batch, batch + 4):
                h = g * 8 + j
                s = sbuf[j, 0:n, :]
                new = jnp.max(s, axis=0, keepdims=True)
                if not first:
                    old = high[h]
                    new = jnp.maximum(old, new)
                p = jnp.exp2((s - new) * scale).astype(BF)
                part = nn(val, p)
                acc[h] = part if first else acc[h] * jnp.exp2((old - new) * scale) + part
                high[h] = new

    def attend_pairs(g, ok, place):
        def body(i, _):
            attend(g, [place(2 * i), place(2 * i + 1)], False)
            return 0

        @pl.when(ok)
        def _():
            lax.fori_loop(0, 2, body, 0)

    def attend_middle(g):
        keys[g].row(1)
        first = chip - y - 4
        attend_pairs(g, z >= 1, lambda i: (first + i, first + i))

    def attend_ends(g):
        keys[g].row(0)
        keys[g].row(2)

        def place(i):
            later = (i + 4 - y) // 4
            seen = 1 - later * (1 - z // 2)
            c = chip - y + i - 8 * later
            return seen * c + (1 - seen) * chip, seen * c + (1 - seen) * 16

        attend_pairs(g, (z >= 2) | (y >= 1), place)

    project_rest(1)
    send_keys(1)
    keys[0].forward()
    attend(0, [(chip, chip)], True)
    take_keys(1)
    attend_middle(0)
    keys[1].forward()
    attend_ends(0)
    attend(1, [(chip, chip)], True)
    attend_middle(1)
    attend_ends(1)

    branch = jnp.zeros((1, 256), F32)
    for h in range(16):
        a = acc[h]
        j = h % 8
        branch = branch + a[j : j + 1] / a[8:9]
    ret_out[...] = jnp.broadcast_to(branch, (8, 256))

    def r_copy(dd, c):
        n = dd * 2 + c
        return pltpu.make_async_remote_copy(
            src_ref=ret_out, dst_ref=ret_in.at[d, core],
            send_sem=rs_sem.at[n], recv_sem=rr_sem.at[n],
            device_id=((d + dd) % 4, 2 * chip + (core + c) % 2), device_id_type=MESH,
        )

    def r_arrival(dd, c):
        n = dd * 2 + c
        return pltpu.make_async_remote_copy(
            src_ref=ret_out, dst_ref=ret_in.at[(d - dd + 4) % 4, (core + c) % 2],
            send_sem=rs_sem.at[n], recv_sem=rr_sem.at[n],
            device_id=(d, 2 * chip + 1 - core), device_id_type=MESH,
        )

    for dd, c in q_pairs:
        r_copy(dd, c).start()
    ret_in[d, core] = ret_out[...]
    for dd, c in q_pairs:
        r_arrival(dd, c).wait_recv()

    lane = (d * 64 + core * 32).astype(F32) + rank_col
    lanes = iota((128, 256), 1).astype(F32)
    value = jnp.zeros((128, 256), F32)
    for b in range(4):
        row = ret_in[b, 0][0:1] + ret_in[b, 1][0:1]
        value = value + jnp.where((lanes == lane) & (bin_col == float(b)), row, 0.0)
    score = jnp.sum(value, axis=1, keepdims=True) + residual
    out_ref[...] = jnp.sum(jnp.where(eye, score, 0.0), axis=0, keepdims=True)

    x_copy.wait_send()
    for g in range(2):
        pair(g, core).wait_send()
        weights[g].finish()
        keys[g].finish()
    for dd, c in q_pairs:
        q_copy(dd, c).wait_send()
        r_copy(dd, c).wait_send()
    for g in range(2):
        for dd in range(1, 4):
            k_copy(g, dd).wait_send()


def on_device(
    hidden, queries, norm_gain, key_value_weight, head_weight, head_fold, route, segments
):
    vmem = pl.BlockSpec(memory_space=pltpu.VMEM)
    hbm = pl.BlockSpec(memory_space=pl.ANY)
    dma = pltpu.SemaphoreType.DMA
    out = pl.pallas_call(
        kernel,
        out_shape=jax.ShapeDtypeStruct((1, 128), F32),
        in_specs=[hbm] * 8,
        out_specs=vmem,
        scratch_shapes=[
            pltpu.VMEM((1, 8192), F32),
            pltpu.VMEM((8192,), BF),
            pltpu.VMEM((4096,), BF),
            pltpu.VMEM((2, 128), jnp.int32),
            pltpu.VMEM((1, 4096), jnp.int32),
            pltpu.VMEM((1, 8192), F32),
            pltpu.VMEM((128, 8192), BF),
            pltpu.VMEM((128, 4096), BF),
            pltpu.VMEM((256, 1024), BF),
            pltpu.VMEM((WROWS[0], 128), BF),
            pltpu.VMEM((WROWS[1], 128), BF),
            pltpu.VMEM((32, 256, 256), BF),
            pltpu.VMEM((16, 2 * WROWS[0], 128), BF),
            pltpu.VMEM((16, 2 * WROWS[1], 128), BF),
            pltpu.VMEM((4, 2, 32, 2176), BF),
            pltpu.VMEM((4, 2, 32, 2176), BF),
            pltpu.VMEM((16, 256, 256), BF),
            pltpu.VMEM((2, 4, 2, 32, 256), BF),
            pltpu.VMEM((2, 4, 2, 32, 256), BF),
            pltpu.VMEM((2, 16, 272, 128), BF),
            pltpu.VMEM((17, 256, 128), BF),
            pltpu.VMEM((256, 256), F32),
            pltpu.VMEM((256, 256), BF),
            pltpu.VMEM((256, 256), BF),
            pltpu.VMEM((2, 256, 128), F32),
            pltpu.VMEM((256, 128), F32),
            pltpu.VMEM((16, 1, 256), F32),
            pltpu.VMEM((16, 16, 256), F32),
            pltpu.VMEM((8, 512, 256), F32),
            pltpu.VMEM((8, 256), F32),
            pltpu.VMEM((4, 2, 8, 256), F32),
            dma((8,)),
            dma((2,)), dma((2,)), dma, dma,
            dma((8,)), dma((8,)),
            dma((2, 4)), dma((2, 4)),
            dma((8,)), dma((8,)),
            dma((2, 2, 5, 4)), dma((2, 2, 5, 4)),
            dma((2, 22)), dma((2, 22)),
        ],
        compiler_params=pltpu.CompilerParams(
            collective_id=0, has_side_effects=True, vmem_limit_bytes=62 * 1024 * 1024
        ),
        cost_estimate=pl.CostEstimate(
            flops=10_000_000_000, bytes_accessed=4_000_000, transcendentals=10_000_000
        ),
    )(
        hidden, queries, norm_gain.reshape(1, -1), key_value_weight,
        head_weight, head_fold, route, segments,
    )
    return out.reshape(-1)


def solution(mesh):
    in_specs = (
        P(("dp", "fsdp"), None),
        P(("dp", "fsdp"), None),
        P(),
        P("fsdp", None),
        P(),
        P(),
        P(None, ("dp", "fsdp")),
        P("dp", None),
    )
    out_specs = P(("dp", "fsdp"))
    return jax.shard_map(
        on_device, mesh=mesh, in_specs=in_specs, out_specs=out_specs, check_vma=False
    )
```

```python
import functools

import jax
import jax.numpy as jnp
from jax import lax
from jax.experimental import pallas as pl
from jax.experimental.pallas import tpu as pltpu
from jax.sharding import PartitionSpec as P

MESH = pl.DeviceIdType.MESH
BF = jnp.bfloat16
F32 = jnp.float32
LOG2E = 1.4426950408889634
NEG = -1e30
WROWS = (288, 256)
KPART = ((0, 96), (96, 176))


def nn(a, b):
    return lax.dot_general(a, b, (((1,), (0,)), ((), ())), preferred_element_type=F32)


def nt(a, b):
    return lax.dot_general(a, b, (((1,), (1,)), ((), ())), preferred_element_type=F32)


def iota(shape, axis):
    return lax.broadcasted_iota(jnp.int32, shape, axis)


def kernel(
    hid_hbm, q_hbm, gain_hbm, w_hbm, hw_hbm, fold_hbm, route_hbm, seg_hbm, out_ref,
    gain_ref, hw_ref, fold_ref, route_ref, seg_ref, hw_row, hid, qv, wv, wpair0, wpair1, x3, wg0, wg1, qout, qin, qx, kvout0, kvout1, kvin0, kvin1, win, kext, bias, onehot, onehot_t,
    kacc, vacc, high, acc, sbuf, ret_out, ret_in,
    load_sem, pair_send, pair_recv, xs_sem, xr_sem, qs_sem, qr_sem, ks_sem, kr_sem,
    rs_sem, rr_sem, ws_sem, wr_sem, gs_sem, gr_sem,
):
    kvout, kvin = (kvout0, kvout1), (kvin0, kvin1)
    d = lax.axis_index("dp")
    f = lax.axis_index("fsdp")
    chip = f // 2
    core = f % 2
    y = chip % 4
    z = chip // 4

    def chip_at(par, u, v):
        return (1 - par) * (4 * v + u) + par * (4 * u + v)

    def coords(par):
        return (1 - par) * y + par * z, (1 - par) * z + par * y

    def near(par, du, dv):
        u, v = coords(par)
        return chip_at(par, (u + du + 4) % 4, (v + dv + 4) % 4)

    barrier = pltpu.get_barrier_semaphore()
    peers = [(d, 2 * chip + (1 - core))]
    for dd in range(1, 4):
        for c in range(2):
            peers.append(((d + dd) % 4, 2 * chip + c))
    for du, dv in ((1, 0), (-1, 0), (0, 1), (0, -1), (2, 0), (0, 2)):
        peers.append((d, 2 * near(0, du, dv) + core))
    for peer in peers:
        pl.semaphore_signal(barrier, inc=1, device_id=peer, device_id_type=MESH)

    loads = [
        pltpu.make_async_copy(src, dst, load_sem.at[n])
        for n, (src, dst) in enumerate([
            (w_hbm, wv), (fold_hbm, fold_ref), (route_hbm, route_ref), (q_hbm, qv),
            (hid_hbm, hid), (hw_hbm, hw_ref), (gain_hbm, gain_ref), (seg_hbm, seg_ref),
        ])
    ]
    load_w, load_fold, load_route, load_q, load_h, load_hw, load_gain, load_seg = loads
    for load in loads:
        load.start()

    load_w.wait()
    load_fold.wait()
    fold = fold_ref[...].reshape(1, 4096).astype(F32)
    head_row = jnp.concatenate(
        [fold[:, h * 128 : (h + 1) * 128] for h in range(32)], axis=0
    )
    fold_t = jnp.concatenate([head_row] * 4, axis=1)
    fold_t = jnp.where(iota((32, 512), 0) // 8 == iota((32, 512), 1) // 128, fold_t, 0.0).astype(BF)
    wf = nt(fold_t, wv[:, 512:1024])
    own_is_1 = core == 1

    def pick(a, b):
        return jnp.where(own_is_1, b, a), jnp.where(own_is_1, a, b)

    packs = [wf[16 * c : 16 * c + 16].astype(BF) for c in range(2)]
    mine, theirs = pick(packs[0], packs[1])
    base = pl.multiple_of(core * WROWS[0], 32)
    for side in range(2):
        at = 256 + 16 * side
        wg0[chip, pl.ds(base + at, 16), :] = mine[:, side * 128 : (side + 1) * 128]
        wpair0[at : at + 16, :] = theirs[:, side * 128 : (side + 1) * 128]
    for g, (wg, wpair) in enumerate(((wg0, wpair0), (wg1, wpair1))):
        mine, theirs = pick(wv[:, g * 128 : g * 128 + 128], wv[:, g * 128 + 256 : g * 128 + 384])
        wg[chip, pl.ds(pl.multiple_of(core * WROWS[g], 32), 256), :] = mine
        wpair[0:256, :] = theirs

    pl.semaphore_wait(barrier, len(peers))

    def pair(g, side):
        at = pl.ds(pl.multiple_of(side * WROWS[g], 32), WROWS[g])
        return pltpu.make_async_remote_copy(
            src_ref=(wpair0, wpair1)[g], dst_ref=(wg0, wg1)[g].at[chip, at],
            send_sem=pair_send.at[g], recv_sem=pair_recv.at[g],
            device_id=(d, 2 * chip + 1 - core), device_id_type=MESH,
        )

    for g in range(2):
        pair(g, core).start()

    class Gather:
        def __init__(self, g):
            self.g, self.half, self.cut = g, WROWS[g], WROWS[g] // 2

        def part(self, par, kind):
            if kind < 2:
                off, n = 0, self.half
            elif kind == 2:
                off, n = 0, self.cut
            else:
                off, n = self.cut, self.half - self.cut
            return pl.ds(pl.multiple_of(par * self.half + off, 16), n)

        def copy(self, par, group, kind, incoming):
            step = 1 if kind in (0, 2) else -1
            hops = (1 if kind < 2 else 2) if incoming else (0 if kind < 2 else 1)
            back = -step * hops
            if group == 0:
                at = near(par, back, 0)
                to = near(par, step, 0)
            else:
                du = (0, -1, 1, 2)[group - 1]
                at = near(par, du, back)
                to = near(par, 0, step)
            ref = (wg0, wg1)[self.g].at[at, self.part(par, kind)]
            return pltpu.make_async_remote_copy(
                src_ref=ref, dst_ref=ref,
                send_sem=ws_sem.at[self.g, par, group, kind],
                recv_sem=wr_sem.at[self.g, par, group, kind],
                device_id=(d, 2 * to + core), device_id_type=MESH,
            )

        def send(self, par, group, kind):
            self.copy(par, group, kind, False).start()

        def wait(self, par, group, kind):
            self.copy(par, group, kind, True).wait_recv()

        def finish(self):
            for par in range(2):
                for group in range(5):
                    for kind in range(4):
                        self.copy(par, group, kind, False).wait_send()

        def begin(self, par, group):
            self.send(par, group, 0)
            self.send(par, group, 1)

        def step1(self):
            for kind in range(2):
                for par in range(2):
                    self.wait(par, 0, kind)
                    self.send(par, 2 + kind, 0)
                    self.send(par, 2 + kind, 1)
                    self.send(par, 0, 2 + kind)

        def step2(self):
            for kind in range(2):
                for par in range(2):
                    self.wait(par, 1, kind)
                    self.send(par, 1, 2 + kind)

        def step3(self):
            for par in range(2):
                self.wait(par, 0, 2)
                self.wait(par, 0, 3)
                self.send(par, 4, 0)
                self.send(par, 4, 1)

        def step4(self):
            for group in (2, 3):
                for kind in range(2):
                    for par in range(2):
                        self.wait(par, group, kind)
                        self.send(par, group, 2 + kind)

        def step5(self):
            for kind in range(2):
                for par in range(2):
                    self.wait(par, 4, kind)
                    self.send(par, 4, 2 + kind)

        def step6(self, group):
            for par in range(2):
                self.wait(par, group, 2)
                self.wait(par, group, 3)

    class Keys:
        def __init__(self, g):
            self.g = g

        def copy(self, n, at, par, to):
            ref = win.at[self.g, at, pl.ds(*KPART[par])]
            return pltpu.make_async_remote_copy(
                src_ref=ref, dst_ref=ref,
                send_sem=gs_sem.at[self.g, n], recv_sem=gr_sem.at[self.g, n],
                device_id=(d, 2 * to + core), device_id_type=MESH,
            )

        def first_y(self, e, incoming):
            at = near(0, -e if incoming else 0, 0)
            return self.copy(e - 1, at, 0, near(0, e, 0)), True

        def first_z(self, j, incoming):
            at = near(0, 0, -j if incoming else 0)
            return self.copy(2 + j, at, 1, near(0, 0, j)), (z >= j if incoming else z < 4 - j)

        def then_z(self, k, j, incoming):
            at = near(0, k, -j if incoming else 0)
            ok = z >= j if incoming else z < 4 - j
            if j == 2:
                ok = ok & ((y + k) % 4 >= y)
            return self.copy(5 + 2 * k + j - 1, at, 0, near(0, 0, j)), ok

        def then_y(self, e, j, incoming):
            at = near(0, -e if incoming else 0, -j)
            source = (y - e + 4) % 4 if incoming else y
            target = y if incoming else (y + e) % 4
            ok = z >= j
            if j == 0:
                ok = source < target
            if j == 2:
                ok = ok & (source >= target)
            return self.copy(13 + 3 * j + e - 1, at, 1, near(0, e, 0)), ok

        def run(self, act, made):
            copy, ok = made
            if ok is True:
                act(copy)
            else:
                @pl.when(ok)
                def _():
                    act(copy)

        def send(self, kind, *which):
            self.run(lambda copy: copy.start(), kind(*which, False))

        def wait(self, kind, *which):
            self.run(lambda copy: copy.wait_recv(), kind(*which, True))

        def begin(self):
            for e in (1, 3, 2):
                self.send(self.first_y, e)
            self.send(self.first_z, 1)
            self.send(self.then_z, 0, 1)
            for e in (1, 3, 2):
                self.send(self.then_y, e, 0)
            self.send(self.first_z, 2)
            self.send(self.then_z, 0, 2)

        def forward(self):
            self.wait(self.first_z, 1)
            for e in (1, 3, 2):
                self.send(self.then_y, e, 1)
            for e in (1, 3, 2):
                self.wait(self.first_y, e)
                self.send(self.then_z, 4 - e, 1)
            for e in (1, 3, 2):
                self.send(self.then_z, 4 - e, 2)
            self.wait(self.first_z, 2)
            for e in (1, 3, 2):
                self.send(self.then_y, e, 2)

        def row(self, j):
            for e in (1, 3, 2):
                self.wait(self.then_y, e, j)
            if j:
                for k in range(4):
                    self.wait(self.then_z, k, j)

        def finish(self):
            done = lambda copy: copy.wait_send()
            for e in (1, 2, 3):
                self.run(done, self.first_y(e, False))
                for j in range(3):
                    self.run(done, self.then_y(e, j, False))
            for j in (1, 2):
                self.run(done, self.first_z(j, False))
                for k in range(4):
                    self.run(done, self.then_z(k, j, False))

    weights = [Gather(0), Gather(1)]
    keys = [Keys(0), Keys(1)]

    for g in range(2):
        for group in range(2):
            if g == 0 or group == 0:
                weights[g].begin(core, group)
        pair(g, 1 - core).wait_recv()
        for group in range(2):
            if g == 0 or group == 0:
                weights[g].begin(1 - core, group)

    load_route.wait()
    route = route_ref[...]
    bins = jnp.broadcast_to(route[0:1, :], (128, 128))
    offs = jnp.broadcast_to(route[1:2, :], (128, 128))
    i0 = iota((128, 128), 0)
    i1 = iota((128, 128), 1)
    member = (bins == i0).astype(F32)
    before = (i0 < i1).astype(BF)
    count = nn(member.astype(BF), before)
    rank = jnp.sum(member * count, axis=0, keepdims=True)
    slot = route[0:1, :].astype(F32) * 32.0 + rank
    perm = (jnp.broadcast_to(slot, (128, 128)) == i0.astype(F32)).astype(BF)
    eye = i0 == i1
    off_col = jnp.sum(jnp.where(eye, offs.astype(F32), 0.0), axis=1, keepdims=True)
    bin_col = jnp.sum(jnp.where(eye, bins.astype(F32), 0.0), axis=1, keepdims=True)
    rank_col = jnp.sum(jnp.where(eye, jnp.broadcast_to(rank, (128, 128)), 0.0), axis=1, keepdims=True)

    load_q.wait()
    off_sorted = nn(perm, jnp.broadcast_to(off_col, (128, 128)).astype(BF)).astype(BF)
    for c in range(2):
        for b in range(4):
            qout[b, c, :, 2048:2176] = off_sorted[b * 32 : (b + 1) * 32]

    def sort_q(i, _):
        for c in range(2):
            src = pl.ds(pl.multiple_of(c * 2048 + i * 256, 256), 256)
            dst = pl.ds(pl.multiple_of(i * 256, 256), 256)
            block = nn(perm, qv[:, src]).astype(BF)
            for b in range(4):
                qout[b, c, :, dst] = block[b * 32 : (b + 1) * 32]
        return 0

    lax.fori_loop(0, 8, sort_q, 0, unroll=4)

    def q_copy(dd, c):
        b = (d + dd) % 4
        to = (core + c) % 2
        n = dd * 2 + c
        return pltpu.make_async_remote_copy(
            src_ref=qout.at[b, to], dst_ref=qin.at[d, core],
            send_sem=qs_sem.at[n], recv_sem=qr_sem.at[n],
            device_id=(b, 2 * chip + to), device_id_type=MESH,
        )

    def q_arrival(dd, c):
        n = dd * 2 + c
        return pltpu.make_async_remote_copy(
            src_ref=qout.at[d, core], dst_ref=qin.at[(d - dd + 4) % 4, (core + c) % 2],
            send_sem=qs_sem.at[n], recv_sem=qr_sem.at[n],
            device_id=(d, 2 * chip + 1 - core), device_id_type=MESH,
        )

    q_pairs = [(dd, c) for dd in range(4) for c in range(2) if dd or c]
    for dd, c in q_pairs:
        q_copy(dd, c).start()
    qin[d, core] = qout[d, core]

    weights[0].step1()
    for par in range(2):
        weights[1].begin(par, 1)

    load_h.wait()
    load_hw.wait()
    load_gain.wait()
    load_seg.wait()
    hw_row[...] = hw_ref[...].reshape(1, 8192).astype(F32)

    def squares(i, carry):
        total, dot = carry
        at = pl.ds(pl.multiple_of(i * 256, 256), 256)
        x = hid[:, at].astype(F32)
        return total + x * x, dot + x * hw_row[:, at]

    zero = jnp.zeros((128, 256), F32)
    total, dot = lax.fori_loop(0, 32, squares, (zero, zero), unroll=4)
    root = lax.rsqrt(jnp.sum(total, axis=1, keepdims=True) * (1.0 / 8192.0) + 1e-05)
    residual = jnp.sum(dot, axis=1, keepdims=True)
    weights[0].step2()
    weights[1].step1()
    my_rows = pl.ds(pl.multiple_of(core * 128, 128), 128)

    def normalise(i, _):
        at = pl.ds(pl.multiple_of(i * 256, 256), 256)
        normed = (hid[:, at].astype(F32) * root * gain_ref[:, at]).astype(BF)
        x3[i, my_rows, :] = nn(perm, normed).astype(BF)
        return 0

    lax.fori_loop(0, 32, normalise, 0, unroll=4)
    x_rows = x3.at[:, my_rows, :]
    x_copy = pltpu.make_async_remote_copy(
        src_ref=x_rows, dst_ref=x_rows, send_sem=xs_sem, recv_sem=xr_sem,
        device_id=(d, 2 * chip + 1 - core), device_id_type=MESH,
    )
    other_rows = x3.at[:, pl.ds(pl.multiple_of((1 - core) * 128, 128), 128), :]
    x_in = pltpu.make_async_remote_copy(
        src_ref=other_rows, dst_ref=other_rows, send_sem=xs_sem, recv_sem=xr_sem,
        device_id=(d, 2 * chip + 1 - core), device_id_type=MESH,
    )
    x_copy.start()
    weights[0].step3()
    weights[1].step2()
    weights[0].step4()

    def segment_keys(i, _):
        at = pl.ds(pl.multiple_of(i * 256, 256), 256)
        s = jnp.broadcast_to(seg_ref[:, at], (128, 256))
        k = iota((128, 256), 0)
        part = jnp.where((k < 8) & (s != k), NEG, 0.0)
        kext[i] = part.T.astype(BF)
        return 0

    lax.fori_loop(0, 16, segment_keys, 0, unroll=4)
    kext[16] = jnp.where(iota((256, 128), 1) < 8, NEG, 0.0).astype(BF)

    x_in.wait_recv()
    kacc[...] = jnp.zeros_like(kacc)
    vacc[...] = jnp.zeros_like(vacc)

    def project(g, places):
        wg = (wg0, wg1)[g]
        k_sum = kacc[g]
        v_sum = vacc[:, 0:16]
        for du, dv in places:
            for par in range(2):
                c = near(par, du, dv)
                x = x3[2 * c + par]
                base = par * WROWS[g]
                k_sum += nn(x, wg[c, base : base + 256, :])
                if g == 0:
                    folded = jnp.concatenate(
                        [wg[c, base + 256 : base + 272, :], wg[c, base + 272 : base + 288, :]], axis=1
                    )
                    v_sum += nt(x, folded)
        kacc[g] = k_sum
        if g == 0:
            vacc[:, 0:16] = v_sum

    def project_rest(g):
        for group, place_of in ((1, (0, 2)), (2, (-1, 2)), (3, (1, 2)), (4, (2, 2))):
            weights[g].step6(group)
            project(g, [place_of])

    def send_keys(g):
        k_rows = kacc[g].astype(BF)
        if g == 0:
            v_cols = vacc[...].astype(BF)
        for s in range(2):
            for b in range(4):
                at = s * 128 + b * 32
                kvout[g][b, s, :, 0:128] = k_rows[at : at + 32]
                if g == 0:
                    kvout[0][b, s, :, 128:256] = v_cols[at : at + 32]
        for dd in range(1, 4):
            k_copy(g, dd).start()
        kvin[g][d] = kvout[g][d]

    def take_keys(g):
        for dd in range(1, 4):
            k_arrival(g, dd).wait_recv()
        got_k = kvin[g][:, :, :, 0:128].reshape(256, 128)
        win[g, chip, 0:256, :] = nn(onehot_t[...], got_k).astype(BF)
        if g == 0:
            got_v = kvin[0][:, :, :, 128:256].reshape(256, 128).astype(F32).T[0:16].astype(BF)
            values = nn(got_v, onehot[...])
            for n in range(2):
                of_head = values[8 * n : 8 * n + 8]
                win[n, chip, 256:272, :] = jnp.concatenate(
                    [of_head[:, 0:128], of_head[:, 128:256]], axis=0
                ).astype(BF)
        keys[g].begin()

    def k_copy(g, dd):
        b = (d + dd) % 4
        return pltpu.make_async_remote_copy(
            src_ref=kvout[g].at[b], dst_ref=kvin[g].at[d],
            send_sem=ks_sem.at[g, dd], recv_sem=kr_sem.at[g, dd],
            device_id=(b, f), device_id_type=MESH,
        )

    def k_arrival(g, dd):
        return pltpu.make_async_remote_copy(
            src_ref=kvout[g].at[d], dst_ref=kvin[g].at[(d - dd + 4) % 4],
            send_sem=ks_sem.at[g, dd], recv_sem=kr_sem.at[g, dd],
            device_id=((d + dd) % 4, f), device_id_type=MESH,
        )

    project(0, [(0, 0), (-1, 0), (1, 0)])
    weights[0].step5()
    weights[1].step3()
    project(0, [(0, -1), (0, 1), (2, 0)])
    weights[1].step4()
    project(0, [(-1, -1), (-1, 1), (1, -1)])
    project(0, [(1, 1), (2, -1), (2, 1)])
    project_rest(0)
    send_keys(0)
    weights[1].step5()
    project(1, [(0, 0), (-1, 0), (1, 0)])
    project(1, [(0, -1), (0, 1), (2, 0)])

    for dd, c in q_pairs:
        q_arrival(dd, c).wait_recv()
    off = qin[:, :, :, 2048:2176].reshape(256, 128).astype(F32)
    arrival = iota((256, 128), 0)
    place = off + ((arrival // 32) % 2).astype(F32) * 128.0
    place = jnp.concatenate([place, place], axis=1)
    hot = (place == iota((256, 256), 1).astype(F32)).astype(F32)
    onehot[...] = hot.astype(BF)
    onehot_t[...] = hot.T.astype(BF)
    take_keys(0)
    own_at = pl.ds(pl.multiple_of(chip * 256, 256), 256)
    seg_hot = (jnp.broadcast_to(seg_ref[:, own_at], (128, 256)) == iota((128, 256), 0)).astype(BF)
    qseg = nt(seg_hot, onehot[...]).astype(BF)
    later = jnp.where(iota((256, 256), 0) > iota((256, 256), 1), NEG, 0.0).astype(BF)
    bias[...] = nt(later, onehot[...])
    for h in range(16):
        qh = qin[:, :, :, h * 128 : (h + 1) * 128].reshape(256, 128)
        qx[h, 0:128, :] = qh.astype(F32).T.astype(BF)
        qx[h, 128:256, :] = qseg

    project(1, [(-1, -1), (-1, 1), (1, -1)])
    project(1, [(1, 1), (2, -1), (2, 1)])
    scale = LOG2E * 128.0 ** -0.5

    def attend(g, chunks, first):
        n = 256 * len(chunks)
        values = [win[g, c, 256:272, :].astype(F32) for c, e in chunks]
        values = jnp.concatenate([v[at : at + 8] for v in values for at in (0, 8)], axis=1)
        val = jnp.concatenate([values, jnp.ones((8, n), F32)], axis=0).astype(BF)

        def scores(j):
            key = jnp.concatenate(
                [jnp.concatenate([win[g, c, 0:256, :], kext[e]], axis=1) for c, e in chunks], axis=0
            )
            s = nn(key, qx[g * 8 + j])
            sbuf[j, 0:n, :] = s + bias[...] if first else s

        for j in range(4):
            scores(j)
        for batch in (0, 4):
            if batch == 0:
                for j in range(4, 8):
                    scores(j)
            for j in range(batch, batch + 4):
                h = g * 8 + j
                s = sbuf[j, 0:n, :]
                new = jnp.max(s, axis=0, keepdims=True)
                if not first:
                    old = high[h]
                    new = jnp.maximum(old, new)
                p = jnp.exp2((s - new) * scale).astype(BF)
                part = nn(val, p)
                acc[h] = part if first else acc[h] * jnp.exp2((old - new) * scale) + part
                high[h] = new

    def attend_pairs(g, ok, place):
        def body(i, _):
            attend(g, [place(2 * i), place(2 * i + 1)], False)
            return 0

        @pl.when(ok)
        def _():
            lax.fori_loop(0, 2, body, 0)

    def attend_middle(g):
        keys[g].row(1)
        first = chip - y - 4
        attend_pairs(g, z >= 1, lambda i: (first + i, first + i))

    def attend_ends(g):
        keys[g].row(0)
        keys[g].row(2)

        def place(i):
            later = (i + 4 - y) // 4
            seen = 1 - later * (1 - z // 2)
            c = chip - y + i - 8 * later
            return seen * c + (1 - seen) * chip, seen * c + (1 - seen) * 16

        attend_pairs(g, (z >= 2) | (y >= 1), place)

    project_rest(1)
    send_keys(1)
    keys[0].forward()
    attend(0, [(chip, chip)], True)
    take_keys(1)
    attend_middle(0)
    keys[1].forward()
    attend_ends(0)
    attend(1, [(chip, chip)], True)
    attend_middle(1)
    attend_ends(1)

    branch = jnp.zeros((1, 256), F32)
    for h in range(16):
        a = acc[h]
        j = h % 8
        branch = branch + a[j : j + 1] / a[8:9]
    ret_out[...] = jnp.broadcast_to(branch, (8, 256))

    def r_copy(dd, c):
        n = dd * 2 + c
        return pltpu.make_async_remote_copy(
            src_ref=ret_out, dst_ref=ret_in.at[d, core],
            send_sem=rs_sem.at[n], recv_sem=rr_sem.at[n],
            device_id=((d + dd) % 4, 2 * chip + (core + c) % 2), device_id_type=MESH,
        )

    def r_arrival(dd, c):
        n = dd * 2 + c
        return pltpu.make_async_remote_copy(
            src_ref=ret_out, dst_ref=ret_in.at[(d - dd + 4) % 4, (core + c) % 2],
            send_sem=rs_sem.at[n], recv_sem=rr_sem.at[n],
            device_id=(d, 2 * chip + 1 - core), device_id_type=MESH,
        )

    for dd, c in q_pairs:
        r_copy(dd, c).start()
    ret_in[d, core] = ret_out[...]
    x_copy.wait_send()
    for g in range(2):
        pair(g, core).wait_send()
        weights[g].finish()
        keys[g].finish()
    for dd, c in q_pairs:
        q_copy(dd, c).wait_send()
    for g in range(2):
        for dd in range(1, 4):
            k_copy(g, dd).wait_send()
    for dd, c in q_pairs:
        r_arrival(dd, c).wait_recv()
    for dd, c in q_pairs:
        r_copy(dd, c).wait_send()

    lane = (d * 64 + core * 32).astype(F32) + rank_col
    lanes = iota((128, 256), 1).astype(F32)
    value = jnp.zeros((128, 256), F32)
    for b in range(4):
        row = ret_in[b, 0][0:1] + ret_in[b, 1][0:1]
        value = value + jnp.where((lanes == lane) & (bin_col == float(b)), row, 0.0)
    score = jnp.sum(value, axis=1, keepdims=True) + residual
    out_ref[...] = jnp.sum(jnp.where(eye, score, 0.0), axis=0, keepdims=True)


def on_device(
    hidden, queries, norm_gain, key_value_weight, head_weight, head_fold, route, segments
):
    vmem = pl.BlockSpec(memory_space=pltpu.VMEM)
    hbm = pl.BlockSpec(memory_space=pl.ANY)
    dma = pltpu.SemaphoreType.DMA
    out = pl.pallas_call(
        kernel,
        out_shape=jax.ShapeDtypeStruct((1, 128), F32),
        in_specs=[hbm] * 8,
        out_specs=vmem,
        scratch_shapes=[
            pltpu.VMEM((1, 8192), F32),
            pltpu.VMEM((8192,), BF),
            pltpu.VMEM((4096,), BF),
            pltpu.VMEM((2, 128), jnp.int32),
            pltpu.VMEM((1, 4096), jnp.int32),
            pltpu.VMEM((1, 8192), F32),
            pltpu.VMEM((128, 8192), BF),
            pltpu.VMEM((128, 4096), BF),
            pltpu.VMEM((256, 1024), BF),
            pltpu.VMEM((WROWS[0], 128), BF),
            pltpu.VMEM((WROWS[1], 128), BF),
            pltpu.VMEM((32, 256, 256), BF),
            pltpu.VMEM((16, 2 * WROWS[0], 128), BF),
            pltpu.VMEM((16, 2 * WROWS[1], 128), BF),
            pltpu.VMEM((4, 2, 32, 2176), BF),
            pltpu.VMEM((4, 2, 32, 2176), BF),
            pltpu.VMEM((16, 256, 256), BF),
            pltpu.VMEM((4, 2, 32, 256), BF),
            pltpu.VMEM((4, 2, 32, 128), BF),
            pltpu.VMEM((4, 2, 32, 256), BF),
            pltpu.VMEM((4, 2, 32, 128), BF),
            pltpu.VMEM((2, 16, 272, 128), BF),
            pltpu.VMEM((17, 256, 128), BF),
            pltpu.VMEM((256, 256), F32),
            pltpu.VMEM((256, 256), BF),
            pltpu.VMEM((256, 256), BF),
            pltpu.VMEM((2, 256, 128), F32),
            pltpu.VMEM((256, 128), F32),
            pltpu.VMEM((16, 1, 256), F32),
            pltpu.VMEM((16, 16, 256), F32),
            pltpu.VMEM((8, 512, 256), F32),
            pltpu.VMEM((8, 256), F32),
            pltpu.VMEM((4, 2, 8, 256), F32),
            dma((8,)),
            dma((2,)), dma((2,)), dma, dma,
            dma((8,)), dma((8,)),
            dma((2, 4)), dma((2, 4)),
            dma((8,)), dma((8,)),
            dma((2, 2, 5, 4)), dma((2, 2, 5, 4)),
            dma((2, 22)), dma((2, 22)),
        ],
        compiler_params=pltpu.CompilerParams(
            collective_id=0, has_side_effects=True, vmem_limit_bytes=62 * 1024 * 1024
        ),
        cost_estimate=pl.CostEstimate(
            flops=10_000_000_000, bytes_accessed=4_000_000, transcendentals=10_000_000
        ),
    )(
        hidden, queries, norm_gain.reshape(1, -1), key_value_weight,
        head_weight, head_fold, route, segments,
    )
    return out.reshape(-1)


def solution(mesh):
    in_specs = (
        P(("dp", "fsdp"), None),
        P(("dp", "fsdp"), None),
        P(),
        P("fsdp", None),
        P(),
        P(),
        P(None, ("dp", "fsdp")),
        P("dp", None),
    )
    out_specs = P(("dp", "fsdp"))
    return jax.shard_map(
        on_device, mesh=mesh, in_specs=in_specs, out_specs=out_specs, check_vma=False
    )
```
